128 devices in a mesh: region: 16 (over x, z), sub: 8 (over y, core).
Axes of the slice: x: 4, y: 4, z: 4, core: 2. Of those that a mesh axis runs over, the one named last changes fastest.
Arguments:
- state: bfloat16 [524288, 256], P(('region', 'sub')), may hold values from -0.94921875 to 0.94921875
- grad_out: float32 [524288, 256], P(('region', 'sub')), may hold values from -8 to 8
- weight: bfloat16 [256, 256], replicated, may hold values from -0.375 to 0.375
- tiles: bfloat16 [24576, 128, 128], P(('region', 'sub')), may hold values from -0.25 to 0.25
- tile_row: int32 [24576], P(('region', 'sub')), may hold values from 0 to 31
- tile_col: int32 [24576], P(('region', 'sub')), may hold values from 0 to 39
- send_rows: int32 [128, 4, 256], P(('region', 'sub')), may hold values from 0 to 4095
Outputs:
- adjoint: float32 [524288, 256], P(('region', 'sub'))
- residual_norms: float32 [3], replicated
The draws below stay inside these ranges and needn't reach their ends.
All inputs are finite; a program needn't handle non-finite values.
Results may differ from the reference program's by a relative error of at most 0.009.
Values sent between devices are 32-bit elements; how exact they have to be, the bound alone decides.
No kernel may reach another device: no remote copies, remote signals or barrier semaphores. Data moves between devices by JAX's collectives and lax.ppermute only.
A program may use at most 192 MiB of HBM per device.

```python
import jax
import jax.numpy as jnp
from jax import lax

H = 256
ROWS_DEV = 4096
TILES_DEV = 192
GHOST = 256
NEIGH = 4
ITERS = 3
ROWS = 524288
N_REGION = 16
N_SUB = 8


def draw_grad_out(key, part):
    key = jax.random.fold_in(key, 11)
    noise_key = jax.random.fold_in(key, 0)
    position = jnp.arange(ROWS, dtype=jnp.float32)[:, None] / ROWS
    rising = 0.6 + 1.2 * position
    values = jax.random.truncated_normal(noise_key, -4.0, 4.0, (ROWS, H), jnp.float32)
    return values * rising


def with_ends(array, rng, smallest, high):
    dims = array.shape
    index_at = [jax.random.randint(jax.random.fold_in(rng, axis), (), 0, dims[axis]) for axis in range(len(dims))]
    array = array.at[tuple(index_at)].set(smallest)
    longest = dims.index(max(dims))
    index_at[longest] = (index_at[longest] + 1) % dims[longest]
    return array.at[tuple(index_at)].set(high)


def block_levels(stream_key, extent, shards, smallest, high):
    def one(dim, parts):
        heights = jax.random.uniform(jax.random.fold_in(jax.random.fold_in(stream_key, 6), dim), (parts,), jnp.float32, smallest / len(shards), high / len(shards))
        return jnp.repeat(jnp.exp(heights), extent[dim] // parts).reshape((-1,) + (1,) * (len(extent) - dim - 1))

    level = one(*shards[0])
    for cut in shards[1:]:
        level = level * one(*cut)
    return level


def centred(stream_key, shape, deviation, bound, cuts=(), held_as=jnp.bfloat16):
    factor_of = block_levels(stream_key, shape, cuts, -0.22, 0.18) if cuts else 1.0
    drawn = jax.random.normal(stream_key, shape, jnp.float32) * deviation * factor_of
    return jnp.minimum(jnp.maximum(drawn, -bound), bound).astype(held_as)


def setup_inputs(seed: int = 0) -> dict:
    splits = jax.random.split(jax.random.key(seed), 8)
    return {
        "state": jnp.clip(jax.random.uniform(splits[0], (ROWS, H), jnp.float32, -0.94921875, 0.94921875) * block_levels(splits[0], (ROWS, H), ((0, 128),), -0.4, 0.0), -0.94921875, 0.94921875).astype(jnp.bfloat16),
        "grad_out": draw_grad_out(jax.random.fold_in(splits[7], 71), 0),
        "weight": centred(splits[2], (H, H), H ** -0.5, 0.375),
        "tiles": centred(splits[3], (TILES_DEV * N_REGION * N_SUB, 128, 128), 0.045, 0.25, ((0, 128),)),
        "tile_row": with_ends(jax.random.randint(splits[4], (TILES_DEV * N_REGION * N_SUB,), 0, ROWS_DEV // 128), jax.random.fold_in(splits[4], 1), 0, (ROWS_DEV // 128) - 1).astype(jnp.int32),
        "tile_col": with_ends(jax.random.randint(splits[5], (TILES_DEV * N_REGION * N_SUB,), 0, ROWS_DEV // 128 + NEIGH * GHOST // 128), jax.random.fold_in(splits[5], 1), 0, (ROWS_DEV // 128 + NEIGH * GHOST // 128) - 1).astype(jnp.int32),
        "send_rows": with_ends(jax.random.randint(splits[6], (N_REGION * N_SUB, NEIGH, GHOST), 0, ROWS_DEV), jax.random.fold_in(splits[6], 1), 0, ROWS_DEV - 1).astype(jnp.int32),
    }


def reference(state, grad_out, weight, tiles, tile_row, tile_col, send_rows):
    device_count = N_REGION * N_SUB
    block_count = ROWS_DEV // 128
    extended = block_count + NEIGH * GHOST // 128
    damping = 1.0 - jnp.square(state.astype(jnp.float32))
    tile_grid = tiles.reshape(device_count, TILES_DEV, 128, 128)
    row_grid = tile_row.reshape(device_count, TILES_DEV)
    col_grid = tile_col.reshape(device_count, TILES_DEV)
    directions = jnp.arange(NEIGH, dtype=jnp.int32)

    def aggregate(mixed):
        mixed_grid = mixed.reshape(device_count, block_count, 128, H)

        def visit(total, packed):
            index, tile_part, row_part, col_part, mixed_part = packed
            picked = mixed_part[row_part]
            products = jnp.einsum('tij,tih->tjh', tile_part.astype(jnp.float32), picked.astype(jnp.float32), precision=lax.Precision.HIGHEST)
            summed = jax.ops.segment_sum(products, col_part, num_segments=extended)
            own_part = summed[:block_count].reshape(ROWS_DEV, H)
            offset = (index * ROWS_DEV).astype(jnp.int32)
            current = lax.dynamic_slice_in_dim(total, offset, ROWS_DEV, 0)
            total = lax.dynamic_update_slice_in_dim(total, current + own_part, offset, 0)
            ghosts = summed[block_count:].reshape(NEIGH * GHOST, H)
            region_pos = index // N_SUB
            sub_pos = index % N_SUB
            owners = jnp.stack([(region_pos + 1) % N_REGION * N_SUB + sub_pos, (region_pos + N_REGION - 1) % N_REGION * N_SUB + sub_pos, region_pos * N_SUB + (sub_pos + 1) % N_SUB, region_pos * N_SUB + (sub_pos + N_SUB - 1) % N_SUB]).astype(jnp.int32)
            locals_hit = send_rows[owners, directions]
            places = (owners[:, None] * ROWS_DEV + locals_hit).reshape(-1).astype(jnp.int32)
            total = total.at[places].add(ghosts)
            return (total, None)
        start = jnp.zeros((device_count * ROWS_DEV, H), jnp.float32)
        total, _ = lax.scan(visit, start, (jnp.arange(device_count, dtype=jnp.int32), tile_grid, row_grid, col_grid, mixed_grid))
        return total
    adjoint = grad_out
    norms = []
    for step in range(ITERS):
        scaled = (damping * adjoint).astype(jnp.bfloat16)
        mixed = jnp.dot(scaled, weight.T, preferred_element_type=jnp.float32).astype(jnp.bfloat16)
        updated = grad_out + aggregate(mixed)
        total = jnp.sum(jnp.square(updated - adjoint))
        norms.append(jnp.sqrt(total / (ROWS * H) + 1e-06))
        adjoint = updated
    return (adjoint, jnp.stack(norms))
```

```python
import functools

import jax
import jax.numpy as jnp
from jax import lax
from jax.experimental import pallas as pl
from jax.experimental.pallas import tpu as pltpu
from jax.sharding import PartitionSpec as P

ITERS = 3
B = 128
CHUNK = 512
GROUP = 8
OWN_AT = 256
COUNTS_AT = 512
VMEM_LIMIT = 16 * 1024 * 1024

VMEM = pltpu.VMEM
SMEM = pltpu.SMEM


def vmem_specs(n):
    return [pl.BlockSpec(memory_space=VMEM)] * n


def smem_specs(n):
    return [pl.BlockSpec(memory_space=SMEM)] * n


def kept(x):
    return pltpu.with_memory_space_constraint(x, VMEM)


def mix(adjoint_ref, state_ref, weight_ref, mixed_ref, start):
    rows = pl.ds(start, CHUNK)
    state = state_ref[rows, :].astype(jnp.float32)
    scaled = ((1.0 - state * state) * adjoint_ref[rows, :]).astype(jnp.bfloat16)
    mixed_ref[rows, :] = lax.dot_general(
        scaled, weight_ref[...], (((1,), (1,)), ((), ())), preferred_element_type=jnp.float32
    ).astype(jnp.bfloat16)


def add_tiles(plan_ref, begin, groups, turned_ref, mixed_ref, total_ref, base):
    def group(g, carry):
        parts = []
        for u in range(GROUP):
            entry = plan_ref[begin + g * GROUP + u]
            tile = entry & 255
            row = pl.multiple_of(((entry >> 8) & 255) * B, B)
            col = pl.multiple_of((entry >> 16) * B - base, B)
            parts.append(
                (
                    col,
                    jnp.dot(
                        turned_ref[tile],
                        mixed_ref[pl.ds(row, B), :],
                        preferred_element_type=jnp.float32,
                    ),
                )
            )
        for col, part in parts:
            total_ref[pl.ds(col, B), :] += part
        return carry

    lax.fori_loop(0, groups, group, 0)


def ghosts(plan_ref, slots_ref, turned_ref, mixed_ref, ghost_ref, out_refs, own_blocks):
    ghost_ref[...] = jnp.zeros_like(ghost_ref)
    add_tiles(plan_ref, 0, plan_ref[COUNTS_AT], turned_ref, mixed_ref, ghost_ref, own_blocks * B)
    size = out_refs[0].shape[0]
    for slot, out_ref in enumerate(out_refs):
        at = pl.multiple_of(slots_ref[slot] * size, size)
        out_ref[...] = ghost_ref[pl.ds(at, size), :]


def scatter(adjoint_ref, slots_ref, targets_ref, in_refs):
    size = in_refs[0].shape[0]
    for slot, in_ref in enumerate(in_refs):
        direction = slots_ref[4 + slot]

        def step(g, carry):
            for u in range(8):
                k = g * 8 + u
                row = targets_ref[direction * size + k]
                adjoint_ref[pl.ds(row, 1), :] += in_ref[pl.ds(k, 1), :]
            return carry

        lax.fori_loop(0, size // 8, step, 0)


def first_kernel(
    own_blocks, rows_ref, cols_ref, slots_ref, weight_ref, state_hbm, grad_hbm, tiles_hbm,
    state_ref, grad_ref, turned_ref, mixed_ref, plan_ref, g0, g1, g2, g3,
    tiles_ref, ghost_ref, sems,
):
    tile_count = tiles_hbm.shape[0]
    half = grad_hbm.shape[0] // 2
    loads = []
    for h in range(2):
        at = pl.ds(h * half, half)
        loads.append(pltpu.make_async_copy(state_hbm.at[at], state_ref.at[at], sems.at[2 * h]))
        loads.append(pltpu.make_async_copy(grad_hbm.at[at], grad_ref.at[at], sems.at[2 * h + 1]))
    quarter = tile_count // 4
    for q in range(4):
        at = pl.ds(q * quarter, quarter)
        loads.append(pltpu.make_async_copy(tiles_hbm.at[at], tiles_ref.at[at], sems.at[4 + q]))
    for load in loads:
        load.start()

    def clear(i, carry):
        plan_ref[i] = tile_count + own_blocks * 65536
        plan_ref[OWN_AT + i] = tile_count
        return carry

    lax.fori_loop(0, OWN_AT, clear, 0)

    def place(t, counts):
        ghost_count, own_count = counts
        col = cols_ref[t]
        is_ghost = (col >= own_blocks).astype(jnp.int32)
        at = jnp.where(is_ghost == 1, ghost_count, OWN_AT + own_count)
        plan_ref[at] = t + rows_ref[t] * 256 + col * 65536
        return ghost_count + is_ghost, own_count + 1 - is_ghost

    ghost_count, own_count = lax.fori_loop(0, tile_count, place, (jnp.int32(0), jnp.int32(0)))
    plan_ref[COUNTS_AT] = (ghost_count + GROUP - 1) // GROUP
    plan_ref[COUNTS_AT + 1] = (own_count + GROUP - 1) // GROUP

    for h in range(2):
        loads[2 * h].wait()
        loads[2 * h + 1].wait()

        @pl.loop(0, half // CHUNK)
        def _(i):
            mix(grad_ref, state_ref, weight_ref, mixed_ref,
                pl.multiple_of(h * half + i * CHUNK, CHUNK))

    eye = (
        lax.broadcasted_iota(jnp.int32, (B, B), 0) == lax.broadcasted_iota(jnp.int32, (B, B), 1)
    ).astype(jnp.bfloat16)
    for q in range(4):
        loads[4 + q].wait()

        @pl.loop(0, quarter // 8)
        def _(i):
            for u in range(8):
                t = q * quarter + i * 8 + u
                turned_ref[t] = lax.dot_general(
                    eye, tiles_ref[t], (((1,), (1,)), ((), ())), preferred_element_type=jnp.float32
                ).astype(jnp.bfloat16)

    turned_ref[tile_count] = jnp.zeros((B, B), jnp.bfloat16)
    ghosts(plan_ref, slots_ref, turned_ref, mixed_ref, ghost_ref, (g0, g1, g2, g3), own_blocks)


def own_kernel(measured, plan_ref, turned_ref, mixed_ref, grad_ref, *refs):
    if measured:
        now_ref, before_ref, out_ref, change_ref = refs
        change(now_ref, before_ref, change_ref)
    else:
        (out_ref,) = refs
    out_ref[...] = grad_ref[...]
    add_tiles(
        plan_ref, OWN_AT, plan_ref[COUNTS_AT + 1], turned_ref, mixed_ref, out_ref, 0
    )


def change(now_ref, before_ref, change_ref):
    def step(i, total):
        at = pl.ds(pl.multiple_of(i * 128, 128), 128)
        moved = now_ref[at, :] - before_ref[at, :]
        squares = (moved * moved).reshape(16, 8, 256)
        return total + jnp.sum(squares, axis=0)

    total = lax.fori_loop(
        0, now_ref.shape[0] // 128, step, jnp.zeros((8, 256), jnp.float32)
    )
    change_ref[...] = total[:, :128] + total[:, 128:]


def middle_kernel(
    own_blocks, slots_ref, targets_ref, plan_ref, weight_ref, state_ref, turned_ref, i0, i1, i2, i3, partial_ref,
    adjoint_ref, mixed_ref, g0, g1, g2, g3, ghost_ref,
):
    scatter(adjoint_ref, slots_ref, targets_ref, (i0, i1, i2, i3))

    @pl.loop(0, adjoint_ref.shape[0] // CHUNK)
    def _(i):
        mix(adjoint_ref, state_ref, weight_ref, mixed_ref, pl.multiple_of(i * CHUNK, CHUNK))

    ghosts(plan_ref, slots_ref, turned_ref, mixed_ref, ghost_ref, (g0, g1, g2, g3), own_blocks)


def last_kernel(
    slots_ref, targets_ref, i0, i1, i2, i3, before_ref, change0_ref, change1_ref, partial_ref,
    adjoint_ref, sums_ref, change_ref,
):
    scatter(adjoint_ref, slots_ref, targets_ref, (i0, i1, i2, i3))
    change(adjoint_ref, before_ref, change_ref)
    row = lax.broadcasted_iota(jnp.int32, (8, 128), 0)
    sums = jnp.zeros((8, 128), jnp.float32)
    for i, ref in enumerate((change0_ref, change1_ref, change_ref)):
        sums = jnp.where(row == i, jnp.sum(ref[...]), sums)
    sums_ref[...] = sums


def local(state, grad_out, weight, tiles, tile_row, tile_col, send_rows):
    row_count, feature_count = state.shape
    own_blocks = row_count // B
    region_count = lax.axis_size("region")
    sub_count = lax.axis_size("sub")
    tile_count = tiles.shape[0]
    ghost_count = send_rows.shape[2]
    ghost_rows = send_rows.shape[1] * ghost_count
    f32, bf16, i32 = jnp.float32, jnp.bfloat16, jnp.int32

    region_odd = lax.axis_index("region") % 2
    sub_odd = lax.axis_index("sub") % 2
    slots = jnp.stack(
        [region_odd, 1 - region_odd, 2 + sub_odd, 3 - sub_odd,
         1 - region_odd, region_odd, 3 - sub_odd, 2 + sub_odd]
    ).astype(i32)

    def swap(value, axis, count, odd):
        partner = [(((i + odd) ^ 1) - odd) % count for i in range(count)]
        return lax.ppermute(value, axis, list(enumerate(partner)))

    def exchange(outgoing):
        return (
            swap(outgoing[0], "region", region_count, 0),
            swap(outgoing[1], "region", region_count, 1),
            swap(outgoing[2], "sub", sub_count, 0),
            swap(outgoing[3], "sub", sub_count, 1),
        )

    params = pltpu.CompilerParams(vmem_limit_bytes=VMEM_LIMIT)
    state_k, grad_k, turned, mixed, plan, *outgoing = pl.pallas_call(
        functools.partial(first_kernel, own_blocks),
        in_specs=smem_specs(3) + vmem_specs(1) + [pl.BlockSpec(memory_space=pl.ANY)] * 3,
        out_specs=tuple(vmem_specs(4) + smem_specs(1) + vmem_specs(4)),
        out_shape=(
            VMEM((row_count, feature_count), bf16),
            VMEM((row_count, feature_count), f32),
            VMEM((tile_count + 1, B, B), bf16),
            VMEM((row_count, feature_count), bf16),
            jax.ShapeDtypeStruct((COUNTS_AT + 128,), i32),
        ) + (VMEM((ghost_count, feature_count), f32),) * 4,
        scratch_shapes=[
            VMEM((tile_count, B, B), bf16),
            VMEM((ghost_rows, feature_count), f32),
            pltpu.SemaphoreType.DMA((8,)),
        ],
        compiler_params=params,
        name="first",
    )(tile_row, tile_col, slots, weight, state, grad_out, tiles)
    targets = send_rows.reshape(-1)

    before = None
    adjoint = grad_k
    changes = []
    for step in range(ITERS):
        incoming = exchange(outgoing)
        measured = step > 0
        results = pl.pallas_call(
            functools.partial(own_kernel, measured),
            in_specs=smem_specs(1) + vmem_specs(5 if measured else 3),
            out_specs=tuple(vmem_specs(2 if measured else 1)),
            out_shape=(VMEM((row_count, feature_count), f32),)
            + ((VMEM((8, 128), f32),) if measured else ()),
            compiler_params=params,
            cost_estimate=pl.CostEstimate(flops=10_000_000_000, bytes_accessed=16_000_000, transcendentals=0),
            name="own",
        )(plan, kept(turned), kept(mixed), kept(grad_k), *((kept(adjoint), kept(before)) if measured else ()))
        partial = results[0]
        if measured:
            changes.append(results[1])
        before = adjoint
        incoming = [kept(v) for v in incoming]
        if step < ITERS - 1:
            adjoint, mixed, *outgoing = pl.pallas_call(
                functools.partial(middle_kernel, own_blocks),
                in_specs=smem_specs(3) + vmem_specs(8),
                out_specs=tuple(vmem_specs(6)),
                out_shape=(VMEM((row_count, feature_count), f32), VMEM((row_count, feature_count), bf16))
                + (VMEM((ghost_count, feature_count), f32),) * 4,
                scratch_shapes=[VMEM((ghost_rows, feature_count), f32)],
                input_output_aliases={10: 0},
                compiler_params=params,
                name="middle",
            )(slots, targets, plan, weight, kept(state_k), kept(turned), *incoming, kept(partial))
        else:
            adjoint, sums = pl.pallas_call(
                last_kernel,
                in_specs=smem_specs(2) + vmem_specs(8),
                out_specs=tuple(vmem_specs(2)),
                out_shape=(VMEM((row_count, feature_count), f32), VMEM((8, 128), f32)),
                scratch_shapes=[VMEM((8, 128), f32)],
                input_output_aliases={9: 0},
                compiler_params=params,
                name="last",
            )(slots, targets, *incoming, kept(before), kept(changes[0]), kept(changes[1]), kept(partial))

    def reach(value, axis, count, by):
        return value + lax.ppermute(value, axis, [(i, i ^ by) for i in range(count)])

    for by in (1, 2, 6):
        sums = reach(sums, "sub", sub_count, by)
    for by in (1, 3, 4, 12):
        sums = reach(sums, "region", region_count, by)
    inverse_count = 1.0 / (region_count * sub_count * row_count * feature_count)
    residual_norms = jnp.sqrt(sums[:ITERS, 0] * inverse_count + 1e-06)
    return adjoint, residual_norms


def solution(mesh):
    placed = (
        P(("region", "sub"), None),
        P(("region", "sub"), None),
        P(),
        P(("region", "sub"), None, None),
        P(("region", "sub")),
        P(("region", "sub")),
        P(("region", "sub"), None, None),
    )
    return jax.shard_map(
        local,
        mesh=mesh,
        in_specs=placed,
        out_specs=(P(("region", "sub"), None), P()),
        check_vma=False,
    )
```

```python
import functools

import jax
import jax.numpy as jnp
from jax import lax
from jax.experimental import pallas as pl
from jax.experimental.pallas import tpu as pltpu
from jax.sharding import PartitionSpec as P

ITERS = 3
B = 128
CHUNK = 1024
GROUP = 16
OWN_AT = 256
COUNTS_AT = 512
VMEM_LIMIT = 16 * 1024 * 1024

VMEM = pltpu.VMEM
SMEM = pltpu.SMEM


def vmem_specs(n):
    return [pl.BlockSpec(memory_space=VMEM)] * n


def smem_specs(n):
    return [pl.BlockSpec(memory_space=SMEM)] * n


def in_hbm(x):
    return pltpu.with_memory_space_constraint(x, pltpu.HBM)


def kept(x):
    return pltpu.with_memory_space_constraint(x, VMEM)


def mix(adjoint, state_ref, weight_ref, mixed_ref, rows):
    state = state_ref[rows, :].astype(jnp.float32)
    scaled = ((1.0 - state * state) * adjoint).astype(jnp.bfloat16)
    mixed_ref[rows, :] = lax.dot_general(
        scaled, weight_ref[...], (((1,), (1,)), ((), ())), preferred_element_type=jnp.float32
    ).astype(jnp.bfloat16)


def chunks(row_count):
    def over(body):
        @pl.loop(0, row_count // CHUNK)
        def _(i):
            body(pl.ds(pl.multiple_of(i * CHUNK, CHUNK), CHUNK))

    return over


def add_tiles(plan_ref, begin, groups, tiles_ref, mixed_ref, total_ref, base):
    def group(g, carry):
        parts = []
        for u in range(GROUP):
            entry = plan_ref[begin + g * GROUP + u]
            tile = entry & 255
            row = pl.multiple_of(((entry >> 8) & 255) * B, B)
            col = pl.multiple_of((entry >> 16) * B - base, B)
            part = lax.dot_general(
                tiles_ref[tile], mixed_ref[pl.ds(row, B), :], (((0,), (0,)), ((), ())),
                preferred_element_type=jnp.float32,
            )
            parts.append((col, part))
        for col, part in parts:
            total_ref[pl.ds(col, B), :] += part
        return carry

    lax.fori_loop(0, groups, group, 0)


def ghosts(plan_ref, slots_ref, tiles_ref, mixed_ref, ghost_ref, out_refs, own_blocks):
    ghost_ref[...] = jnp.zeros_like(ghost_ref)
    add_tiles(plan_ref, 0, plan_ref[COUNTS_AT], tiles_ref, mixed_ref, ghost_ref, own_blocks * B)
    size = out_refs[0].shape[0]
    for slot, out_ref in enumerate(out_refs):
        at = pl.multiple_of(slots_ref[slot] * size, size)
        out_ref[...] = ghost_ref[pl.ds(at, size), :]


def gather_incoming(in_refs, incoming_ref):
    size = in_refs[0].shape[0]
    for slot, in_ref in enumerate(in_refs):
        incoming_ref[slot * size:(slot + 1) * size, :] = in_ref[...].astype(jnp.bfloat16)


def first_kernel(
    own_blocks, slots_ref, rows_hbm, cols_hbm, weight_hbm, state_hbm, grad_hbm, tiles_hbm,
    weight_ref, state_ref, grad_ref, tiles_ref, mixed_ref, plan_ref, g0, g1, g2, g3,
    rows_ref, cols_ref, ghost_ref, sems,
):
    tile_count = tiles_hbm.shape[0]
    row_count = grad_hbm.shape[0]
    copies = [
        pltpu.make_async_copy(rows_hbm, rows_ref, sems.at[0]),
        pltpu.make_async_copy(cols_hbm, cols_ref, sems.at[1]),
        pltpu.make_async_copy(weight_hbm, weight_ref, sems.at[2]),
    ]
    parts = row_count // CHUNK
    for p in range(parts):
        at = pl.ds(p * CHUNK, CHUNK)
        copies.append(pltpu.make_async_copy(state_hbm.at[at], state_ref.at[at], sems.at[3 + 2 * p]))
        copies.append(pltpu.make_async_copy(grad_hbm.at[at], grad_ref.at[at], sems.at[4 + 2 * p]))
    copies.append(
        pltpu.make_async_copy(tiles_hbm, tiles_ref.at[pl.ds(0, tile_count)], sems.at[3 + 2 * parts])
    )
    for copy in copies:
        copy.start()
    tiles_ref[tile_count] = jnp.zeros((B, B), jnp.bfloat16)
    copies[0].wait()
    copies[1].wait()

    def place(g, counts):
        ghost_count, own_count = counts
        for u in range(4):
            t = g * 4 + u
            col = cols_ref[t]
            is_ghost = (col >= own_blocks).astype(jnp.int32)
            at = jnp.where(is_ghost == 1, ghost_count, OWN_AT + own_count)
            plan_ref[at] = t + rows_ref[t] * 256 + col * 65536
            ghost_count = ghost_count + is_ghost
            own_count = own_count + 1 - is_ghost
        return ghost_count, own_count

    ghost_count, own_count = lax.fori_loop(
        0, tile_count // 4, place, (jnp.int32(0), jnp.int32(0))
    )
    for u in range(GROUP):
        plan_ref[ghost_count + u] = tile_count + own_blocks * 65536
        plan_ref[OWN_AT + own_count + u] = tile_count
    plan_ref[COUNTS_AT] = (ghost_count + GROUP - 1) // GROUP
    plan_ref[COUNTS_AT + 1] = (own_count + GROUP - 1) // GROUP

    copies[2].wait()
    for p in range(parts):
        copies[3 + 2 * p].wait()
        copies[4 + 2 * p].wait()
        at = pl.ds(p * CHUNK, CHUNK)
        mix(grad_ref[at, :], state_ref, weight_ref, mixed_ref, at)
    copies[-1].wait()
    ghosts(plan_ref, slots_ref, tiles_ref, mixed_ref, ghost_ref, (g0, g1, g2, g3), own_blocks)


def first_own_kernel(
    plan_ref, slots_ref, targets_ref, tiles_ref, mixed_ref, grad_ref, out_ref, route_ref
):
    size = targets_ref.shape[1]
    row_count = grad_ref.shape[0]
    for slot in range(4):
        target = targets_ref[pl.ds(slots_ref[4 + slot], 1), :]

        @pl.loop(0, row_count // 128)
        def _(i):
            at = pl.multiple_of(i * 128, 128)
            agent = lax.broadcasted_iota(jnp.int32, (128, size), 0) + at
            route_ref[pl.ds(at, 128), slot * size:(slot + 1) * size] = jnp.where(
                agent == target, 1.0, 0.0
            ).astype(jnp.bfloat16)

    out_ref[...] = grad_ref[...]
    add_tiles(plan_ref, OWN_AT, plan_ref[COUNTS_AT + 1], tiles_ref, mixed_ref, out_ref, 0)


def own_kernel(plan_ref, tiles_ref, mixed_ref, grad_ref, now_ref, before_ref, out_ref, change_ref):
    change_ref[...] = jnp.zeros_like(change_ref)
    over = chunks(now_ref.shape[0])

    @over
    def _(rows):
        change_ref[...] += squares(now_ref[rows, :] - before_ref[rows, :])

    out_ref[...] = grad_ref[...]
    add_tiles(plan_ref, OWN_AT, plan_ref[COUNTS_AT + 1], tiles_ref, mixed_ref, out_ref, 0)


def squares(moved):
    total = jnp.sum((moved * moved).reshape(-1, 8, moved.shape[1]), axis=0)
    return total[:, :128] + total[:, 128:]


def middle_kernel(
    own_blocks, slots_ref, plan_ref, weight_ref, state_ref, tiles_ref, route_ref, i0, i1, i2, i3,
    partial_ref, adjoint_ref, mixed_ref, g0, g1, g2, g3, incoming_ref, ghost_ref,
):
    gather_incoming((i0, i1, i2, i3), incoming_ref)
    over = chunks(adjoint_ref.shape[0])

    @over
    def _(rows):
        adjoint = partial_ref[rows, :] + jnp.dot(
            route_ref[rows, :], incoming_ref[...], preferred_element_type=jnp.float32
        )
        adjoint_ref[rows, :] = adjoint
        mix(adjoint, state_ref, weight_ref, mixed_ref, rows)

    ghosts(plan_ref, slots_ref, tiles_ref, mixed_ref, ghost_ref, (g0, g1, g2, g3), own_blocks)


def last_kernel(
    route_ref, i0, i1, i2, i3, before_ref, change0_ref, change1_ref, partial_ref,
    adjoint_ref, sums_ref, incoming_ref, change_ref,
):
    gather_incoming((i0, i1, i2, i3), incoming_ref)
    change_ref[...] = jnp.zeros_like(change_ref)
    over = chunks(adjoint_ref.shape[0])

    @over
    def _(rows):
        adjoint = partial_ref[rows, :] + jnp.dot(
            route_ref[rows, :], incoming_ref[...], preferred_element_type=jnp.float32
        )
        adjoint_ref[rows, :] = adjoint
        change_ref[...] += squares(adjoint - before_ref[rows, :])

    row = lax.broadcasted_iota(jnp.int32, (8, 128), 0)
    sums = jnp.zeros((8, 128), jnp.float32)
    for i, ref in enumerate((change0_ref, change1_ref, change_ref)):
        sums = jnp.where(row == i, jnp.sum(ref[...]), sums)
    sums_ref[...] = sums


def local(state, grad_out, weight, tiles, tile_row, tile_col, send_rows):
    row_count, feature_count = state.shape
    own_blocks = row_count // B
    region_count = lax.axis_size("region")
    sub_count = lax.axis_size("sub")
    tile_count = tiles.shape[0]
    ghost_count = send_rows.shape[2]
    ghost_rows = send_rows.shape[1] * ghost_count
    f32, bf16, i32 = jnp.float32, jnp.bfloat16, jnp.int32

    region_odd = lax.axis_index("region") % 2
    sub_odd = lax.axis_index("sub") % 2
    slots = jnp.stack(
        [region_odd, 1 - region_odd, 2 + sub_odd, 3 - sub_odd,
         1 - region_odd, region_odd, 3 - sub_odd, 2 + sub_odd]
    ).astype(i32)

    def swap(value, axis, count, odd):
        partner = [(((i + odd) ^ 1) - odd) % count for i in range(count)]
        return lax.ppermute(value, axis, list(enumerate(partner)))

    def exchange(outgoing):
        return (
            swap(outgoing[0], "region", region_count, 0),
            swap(outgoing[1], "region", region_count, 1),
            swap(outgoing[2], "sub", sub_count, 0),
            swap(outgoing[3], "sub", sub_count, 1),
        )

    params = pltpu.CompilerParams(vmem_limit_bytes=VMEM_LIMIT)
    beside = pl.CostEstimate(flops=10_000_000_000, bytes_accessed=16_000_000, transcendentals=0)
    parts = row_count // CHUNK
    agents_f32 = VMEM((row_count, feature_count), f32)
    agents_bf16 = VMEM((row_count, feature_count), bf16)
    outgoing_shapes = (VMEM((ghost_count, feature_count), f32),) * 4
    incoming_scratch = VMEM((ghost_rows, feature_count), bf16)
    ghost_scratch = VMEM((ghost_rows, feature_count), f32)

    weight_k, state_k, grad_k, tiles_k, mixed, plan, *outgoing = pl.pallas_call(
        functools.partial(first_kernel, own_blocks),
        in_specs=smem_specs(1) + [pl.BlockSpec(memory_space=pltpu.HBM)] * 6,
        out_specs=tuple(vmem_specs(5) + smem_specs(1) + vmem_specs(4)),
        out_shape=(
            VMEM(weight.shape, bf16),
            agents_bf16,
            agents_f32,
            VMEM((tile_count + 1, B, B), bf16),
            agents_bf16,
            jax.ShapeDtypeStruct((COUNTS_AT + 128,), i32),
        )
        + outgoing_shapes,
        scratch_shapes=[
            SMEM((tile_count,), i32),
            SMEM((tile_count,), i32),
            ghost_scratch,
            pltpu.SemaphoreType.DMA((4 + 2 * parts,)),
        ],
        compiler_params=params,
        name="first",
    )(slots, *[in_hbm(v) for v in (tile_row, tile_col, weight, state, grad_out, tiles)])
    weight_k, state_k, grad_k, tiles_k = [kept(v) for v in (weight_k, state_k, grad_k, tiles_k)]

    before = None
    adjoint = grad_k
    changes = []
    for step in range(ITERS):
        incoming = [kept(v) for v in exchange(outgoing)]
        if step == 0:
            partial, route = pl.pallas_call(
                first_own_kernel,
                in_specs=smem_specs(2) + vmem_specs(4),
                out_specs=tuple(vmem_specs(2)),
                out_shape=(agents_f32, VMEM((row_count, ghost_rows), bf16)),
                compiler_params=params,
                cost_estimate=beside,
                name="first_own",
            )(plan, slots, send_rows.reshape(4, ghost_count), tiles_k, kept(mixed), grad_k)
            route = kept(route)
        else:
            partial, moved = pl.pallas_call(
                own_kernel,
                in_specs=smem_specs(1) + vmem_specs(5),
                out_specs=tuple(vmem_specs(2)),
                out_shape=(agents_f32, VMEM((8, 128), f32)),
                compiler_params=params,
                cost_estimate=beside,
                name="own",
            )(plan, tiles_k, kept(mixed), grad_k, kept(adjoint), kept(before))
            changes.append(kept(moved))
        before = adjoint
        if step < ITERS - 1:
            adjoint, mixed, *outgoing = pl.pallas_call(
                functools.partial(middle_kernel, own_blocks),
                in_specs=smem_specs(2) + vmem_specs(9),
                out_specs=tuple(vmem_specs(6)),
                out_shape=(agents_f32, agents_bf16) + outgoing_shapes,
                scratch_shapes=[incoming_scratch, ghost_scratch],
                input_output_aliases={10: 0},
                compiler_params=params,
                name="middle",
            )(slots, plan, weight_k, state_k, tiles_k, route, *incoming, kept(partial))
        else:
            adjoint, sums = pl.pallas_call(
                last_kernel,
                in_specs=vmem_specs(9),
                out_specs=tuple(vmem_specs(2)),
                out_shape=(agents_f32, VMEM((8, 128), f32)),
                scratch_shapes=[incoming_scratch, VMEM((8, 128), f32)],
                input_output_aliases={8: 0},
                compiler_params=params,
                name="last",
            )(route, *incoming, kept(before), *changes, kept(partial))

    def reach(value, axis, count, by):
        return value + lax.ppermute(value, axis, [(i, i ^ by) for i in range(count)])

    for by in (1, 2, 6):
        sums = reach(sums, "sub", sub_count, by)
    for by in (1, 3, 4, 12):
        sums = reach(sums, "region", region_count, by)
    inverse_count = 1.0 / (region_count * sub_count * row_count * feature_count)
    residual_norms = jnp.sqrt(sums[:ITERS, 0] * inverse_count + 1e-06)
    return adjoint, residual_norms


def solution(mesh):
    placed = (
        P(("region", "sub"), None),
        P(("region", "sub"), None),
        P(),
        P(("region", "sub"), None, None),
        P(("region", "sub")),
        P(("region", "sub")),
        P(("region", "sub"), None, None),
    )
    return jax.shard_map(
        local,
        mesh=mesh,
        in_specs=placed,
        out_specs=(P(("region", "sub"), None), P()),
        check_vma=False,
    )
```

```python
import functools

import jax
import jax.numpy as jnp
from jax import lax
from jax.experimental import pallas as pl
from jax.experimental.pallas import tpu as pltpu
from jax.sharding import PartitionSpec as P

ITERS = 3
B = 128
LOAD = 1024
CHUNK = 2048
OWN_GROUP = 16
GHOST_GROUP = 8
SECOND = 128
OWN_AT = 256
COUNTS_AT = 512
VMEM_LIMIT = 16 * 1024 * 1024

VMEM = pltpu.VMEM
SMEM = pltpu.SMEM


def vmem_specs(n):
    return [pl.BlockSpec(memory_space=VMEM)] * n


def smem_specs(n):
    return [pl.BlockSpec(memory_space=SMEM)] * n


def in_hbm(x):
    return pltpu.with_memory_space_constraint(x, pltpu.HBM)


def kept(x):
    return pltpu.with_memory_space_constraint(x, VMEM)


def mix(adjoint, state_ref, weight_ref, mixed_ref, rows):
    state = state_ref[rows, :].astype(jnp.float32)
    scaled = ((1.0 - state * state) * adjoint).astype(jnp.bfloat16)
    mixed_ref[rows, :] = lax.dot_general(
        scaled, weight_ref[...], (((1,), (1,)), ((), ())), preferred_element_type=jnp.float32
    ).astype(jnp.bfloat16)


def chunks(row_count):
    def over(body):
        @pl.loop(0, row_count // CHUNK)
        def _(i):
            body(pl.ds(pl.multiple_of(i * CHUNK, CHUNK), CHUNK))

    return over


def add_tiles(plan_ref, begin, groups, size, tiles_ref, mixed_ref, total_ref, base):
    def rows_of(entry):
        return mixed_ref[pl.ds(pl.multiple_of(((entry >> 8) & 255) * B, B), B), :]

    def group(g, carry):
        parts = []
        for u in range(size):
            first = plan_ref[begin + g * size + u]
            second = plan_ref[begin + SECOND + g * size + u]
            col = pl.multiple_of((first >> 16) * B - base, B)
            part = lax.dot_general(
                jnp.concatenate([tiles_ref[first & 255], tiles_ref[second & 255]], axis=0),
                jnp.concatenate([rows_of(first), rows_of(second)], axis=0),
                (((0,), (0,)), ((), ())),
                preferred_element_type=jnp.float32,
            )
            parts.append((col, part))
        for col, part in parts:
            total_ref[pl.ds(col, B), :] += part
        return carry

    lax.fori_loop(0, groups, group, 0)


def ghosts(plan_ref, slots_ref, tiles_ref, mixed_ref, ghost_ref, out_refs, own_blocks):
    ghost_ref[...] = jnp.zeros_like(ghost_ref)
    add_tiles(
        plan_ref, 0, plan_ref[COUNTS_AT], GHOST_GROUP, tiles_ref, mixed_ref, ghost_ref, own_blocks * B
    )
    size = out_refs[0].shape[0]
    for slot, out_ref in enumerate(out_refs):
        at = pl.multiple_of(slots_ref[slot] * size, size)
        out_ref[...] = ghost_ref[pl.ds(at, size), :]


def gather_incoming(in_refs, incoming_ref):
    size = in_refs[0].shape[0]
    for slot, in_ref in enumerate(in_refs):
        incoming_ref[slot * size:(slot + 1) * size, :] = in_ref[...].astype(jnp.bfloat16)


def first_kernel(
    own_blocks, slots_ref, rows_hbm, cols_hbm, targets_hbm, weight_hbm, state_hbm, grad_hbm, tiles_hbm,
    weight_ref, state_ref, grad_ref, tiles_ref, mixed_ref, route_ref, plan_ref, g0, g1, g2, g3,
    rows_ref, cols_ref, waiting_ref, targets_ref, ghost_ref, sems,
):
    tile_count = tiles_hbm.shape[0]
    row_count = grad_hbm.shape[0]
    size = targets_hbm.shape[1]
    ghost_blocks = targets_hbm.shape[0] * size // B
    copies = [
        pltpu.make_async_copy(rows_hbm, rows_ref, sems.at[0]),
        pltpu.make_async_copy(cols_hbm, cols_ref, sems.at[1]),
        pltpu.make_async_copy(targets_hbm, targets_ref, sems.at[2]),
        pltpu.make_async_copy(weight_hbm, weight_ref, sems.at[3]),
    ]
    parts = row_count // LOAD
    for p in range(parts):
        at = pl.ds(p * LOAD, LOAD)
        copies.append(pltpu.make_async_copy(state_hbm.at[at], state_ref.at[at], sems.at[4 + 2 * p]))
        copies.append(pltpu.make_async_copy(grad_hbm.at[at], grad_ref.at[at], sems.at[5 + 2 * p]))
    copies.append(
        pltpu.make_async_copy(tiles_hbm, tiles_ref.at[pl.ds(0, tile_count)], sems.at[4 + 2 * parts])
    )
    for copy in copies:
        copy.start()
    tiles_ref[tile_count] = jnp.zeros((B, B), jnp.bfloat16)
    for c in range(own_blocks + ghost_blocks):
        waiting_ref[c] = -1
    for copy in copies[:3]:
        copy.wait()

    steps = tile_count // 3
    band = row_count // steps

    def place(g, counts):
        ghost_count, own_count = counts
        for u in range(3):
            t = g * 3 + u
            col = cols_ref[t]
            entry = t + rows_ref[t] * 256
            other = waiting_ref[col]
            paired = (other >= 0).astype(jnp.int32)
            is_ghost = (col >= own_blocks).astype(jnp.int32)
            at = jnp.where(is_ghost == 1, ghost_count, OWN_AT + own_count)
            plan_ref[at] = entry + col * 65536
            plan_ref[at + SECOND] = other
            waiting_ref[col] = jnp.where(paired == 1, -1, entry)
            ghost_count = ghost_count + is_ghost * paired
            own_count = own_count + (1 - is_ghost) * paired
        rows = pl.ds(pl.multiple_of(g * band, band), band)
        agent = lax.broadcasted_iota(jnp.int32, (band, size), 0) + g * band
        for slot in range(4):
            target = targets_ref[pl.ds(slots_ref[4 + slot], 1), :]
            route_ref[rows, slot * size:(slot + 1) * size] = jnp.where(
                agent == target, 1.0, 0.0
            ).astype(jnp.bfloat16)
        return ghost_count, own_count

    counts = lax.fori_loop(0, steps, place, (jnp.int32(0), jnp.int32(0)))

    def close(begin, blocks, count, group):
        for c in blocks:
            other = waiting_ref[c]
            plan_ref[begin + count] = other + c * 65536
            plan_ref[begin + count + SECOND] = tile_count
            count = count + (other >= 0).astype(jnp.int32)
        for u in range(group):
            plan_ref[begin + count + u] = tile_count + blocks[0] * 65536
            plan_ref[begin + count + u + SECOND] = tile_count
        return (count + group - 1) // group

    all_blocks = list(range(own_blocks + ghost_blocks))
    plan_ref[COUNTS_AT] = close(0, all_blocks[own_blocks:], counts[0], GHOST_GROUP)
    plan_ref[COUNTS_AT + 1] = close(OWN_AT, all_blocks[:own_blocks], counts[1], OWN_GROUP)

    copies[3].wait()
    for p in range(parts):
        copies[4 + 2 * p].wait()
        copies[5 + 2 * p].wait()
        at = pl.ds(p * LOAD, LOAD)
        mix(grad_ref[at, :], state_ref, weight_ref, mixed_ref, at)
    copies[-1].wait()
    ghosts(plan_ref, slots_ref, tiles_ref, mixed_ref, ghost_ref, (g0, g1, g2, g3), own_blocks)


def first_own_kernel(plan_ref, tiles_ref, mixed_ref, grad_ref, out_ref):
    out_ref[...] = grad_ref[...]
    add_tiles(
        plan_ref, OWN_AT, plan_ref[COUNTS_AT + 1], OWN_GROUP, tiles_ref, mixed_ref, out_ref, 0
    )


def own_kernel(plan_ref, tiles_ref, mixed_ref, grad_ref, now_ref, before_ref, out_ref, change_ref):
    change_ref[...] = jnp.zeros_like(change_ref)
    over = chunks(now_ref.shape[0])

    @over
    def _(rows):
        change_ref[...] += squares(now_ref[rows, :] - before_ref[rows, :])

    out_ref[...] = grad_ref[...]
    add_tiles(
        plan_ref, OWN_AT, plan_ref[COUNTS_AT + 1], OWN_GROUP, tiles_ref, mixed_ref, out_ref, 0
    )


def squares(moved):
    total = jnp.sum((moved * moved).reshape(-1, 8, moved.shape[1]), axis=0)
    return total[:, :128] + total[:, 128:]


def middle_kernel(
    own_blocks, slots_ref, plan_ref, weight_ref, state_ref, tiles_ref, route_ref, i0, i1, i2, i3,
    partial_ref, adjoint_ref, mixed_ref, g0, g1, g2, g3, incoming_ref, ghost_ref,
):
    gather_incoming((i0, i1, i2, i3), incoming_ref)
    over = chunks(adjoint_ref.shape[0])

    @over
    def _(rows):
        adjoint = partial_ref[rows, :] + jnp.dot(
            route_ref[rows, :], incoming_ref[...], preferred_element_type=jnp.float32
        )
        adjoint_ref[rows, :] = adjoint
        mix(adjoint, state_ref, weight_ref, mixed_ref, rows)

    ghosts(plan_ref, slots_ref, tiles_ref, mixed_ref, ghost_ref, (g0, g1, g2, g3), own_blocks)


def last_kernel(
    route_ref, i0, i1, i2, i3, before_ref, change0_ref, change1_ref, partial_ref,
    adjoint_hbm, sums_ref, incoming_ref, adjoint_ref, sems,
):
    gather_incoming((i0, i1, i2, i3), incoming_ref)
    row_count = partial_ref.shape[0]
    change = jnp.zeros((8, 128), jnp.float32)
    copies = []
    for p in range(row_count // LOAD):
        rows = pl.ds(p * LOAD, LOAD)
        adjoint = partial_ref[rows, :] + jnp.dot(
            route_ref[rows, :], incoming_ref[...], preferred_element_type=jnp.float32
        )
        adjoint_ref[rows, :] = adjoint
        copies.append(pltpu.make_async_copy(adjoint_ref.at[rows], adjoint_hbm.at[rows], sems.at[p]))
        copies[-1].start()
        change += squares(adjoint - before_ref[rows, :])

    lane = lax.broadcasted_iota(jnp.int32, sums_ref.shape, 1)
    sums = jnp.zeros(sums_ref.shape, jnp.float32)
    for i, value in enumerate((change0_ref[...], change1_ref[...], change)):
        sums = jnp.where(lane == i, jnp.sum(value), sums)
    sums_ref[...] = sums
    for copy in copies:
        copy.wait()


def local(state, grad_out, weight, tiles, tile_row, tile_col, send_rows):
    row_count, feature_count = state.shape
    own_blocks = row_count // B
    region_count = lax.axis_size("region")
    sub_count = lax.axis_size("sub")
    tile_count = tiles.shape[0]
    ghost_count = send_rows.shape[2]
    ghost_rows = send_rows.shape[1] * ghost_count
    f32, bf16, i32 = jnp.float32, jnp.bfloat16, jnp.int32

    region_odd = lax.axis_index("region") % 2
    sub_odd = lax.axis_index("sub") % 2
    slots = jnp.stack(
        [region_odd, 1 - region_odd, 2 + sub_odd, 3 - sub_odd,
         1 - region_odd, region_odd, 3 - sub_odd, 2 + sub_odd]
    ).astype(i32)

    def swap(value, axis, count, odd):
        partner = [(((i + odd) ^ 1) - odd) % count for i in range(count)]
        return lax.ppermute(value, axis, list(enumerate(partner)))

    def exchange(outgoing):
        return (
            swap(outgoing[0], "region", region_count, 0),
            swap(outgoing[1], "region", region_count, 1),
            swap(outgoing[2], "sub", sub_count, 0),
            swap(outgoing[3], "sub", sub_count, 1),
        )

    params = pltpu.CompilerParams(vmem_limit_bytes=VMEM_LIMIT)
    beside = pl.CostEstimate(flops=10_000_000_000, bytes_accessed=16_000_000, transcendentals=0)
    parts = row_count // LOAD
    agents_f32 = VMEM((row_count, feature_count), f32)
    agents_bf16 = VMEM((row_count, feature_count), bf16)
    outgoing_shapes = (VMEM((ghost_count, feature_count), f32),) * 4
    incoming_scratch = VMEM((ghost_rows, feature_count), bf16)
    ghost_scratch = VMEM((ghost_rows, feature_count), f32)

    targets = send_rows.reshape(4, ghost_count)
    weight_k, state_k, grad_k, tiles_k, mixed, route, plan, *outgoing = pl.pallas_call(
        functools.partial(first_kernel, own_blocks),
        in_specs=smem_specs(1) + [pl.BlockSpec(memory_space=pltpu.HBM)] * 7,
        out_specs=tuple(vmem_specs(6) + smem_specs(1) + vmem_specs(4)),
        out_shape=(
            VMEM(weight.shape, bf16),
            agents_bf16,
            agents_f32,
            VMEM((tile_count + 1, B, B), bf16),
            agents_bf16,
            VMEM((row_count, ghost_rows), bf16),
            jax.ShapeDtypeStruct((COUNTS_AT + 128,), i32),
        )
        + outgoing_shapes,
        scratch_shapes=[
            SMEM((tile_count,), i32),
            SMEM((tile_count,), i32),
            SMEM((128,), i32),
            VMEM((4, ghost_count), i32),
            ghost_scratch,
            pltpu.SemaphoreType.DMA((5 + 2 * parts,)),
        ],
        compiler_params=params,
        name="first",
    )(slots, *[in_hbm(v) for v in (tile_row, tile_col, targets, weight, state, grad_out, tiles)])
    weight_k, state_k, grad_k, tiles_k, route = [
        kept(v) for v in (weight_k, state_k, grad_k, tiles_k, route)
    ]

    before = None
    adjoint = grad_k
    changes = []
    for step in range(ITERS):
        incoming = [kept(v) for v in exchange(outgoing)]
        if step == 0:
            (partial,) = pl.pallas_call(
                first_own_kernel,
                in_specs=smem_specs(1) + vmem_specs(3),
                out_specs=tuple(vmem_specs(1)),
                out_shape=(agents_f32,),
                compiler_params=params,
                cost_estimate=beside,
                name="first_own",
            )(plan, tiles_k, kept(mixed), grad_k)
        else:
            partial, moved = pl.pallas_call(
                own_kernel,
                in_specs=smem_specs(1) + vmem_specs(5),
                out_specs=tuple(vmem_specs(2)),
                out_shape=(agents_f32, VMEM((8, 128), f32)),
                compiler_params=params,
                cost_estimate=beside,
                name="own",
            )(plan, tiles_k, kept(mixed), grad_k, kept(adjoint), kept(before))
            changes.append(kept(moved))
        before = adjoint
        if step < ITERS - 1:
            adjoint, mixed, *outgoing = pl.pallas_call(
                functools.partial(middle_kernel, own_blocks),
                in_specs=smem_specs(2) + vmem_specs(9),
                out_specs=tuple(vmem_specs(6)),
                out_shape=(agents_f32, agents_bf16) + outgoing_shapes,
                scratch_shapes=[incoming_scratch, ghost_scratch],
                input_output_aliases={10: 0},
                compiler_params=params,
                name="middle",
            )(slots, plan, weight_k, state_k, tiles_k, route, *incoming, kept(partial))
        else:
            adjoint, sums = pl.pallas_call(
                last_kernel,
                in_specs=vmem_specs(9),
                out_specs=(pl.BlockSpec(memory_space=pltpu.HBM), pl.BlockSpec(memory_space=VMEM)),
                out_shape=(
                    pltpu.HBM((row_count, feature_count), f32),
                    VMEM((region_count * sub_count, 128), f32),
                ),
                scratch_shapes=[incoming_scratch, agents_f32, pltpu.SemaphoreType.DMA((parts,))],
                compiler_params=params,
                name="last",
            )(route, *incoming, kept(before), *changes, kept(partial))

    sums = lax.all_to_all(sums, ("region", "sub"), 0, 0, tiled=True)
    total = jnp.sum(sums, axis=0)
    inverse_count = 1.0 / (region_count * sub_count * row_count * feature_count)
    residual_norms = jnp.sqrt(total[:ITERS] * inverse_count + 1e-06)
    return adjoint, residual_norms


def solution(mesh):
    placed = (
        P(("region", "sub"), None),
        P(("region", "sub"), None),
        P(),
        P(("region", "sub"), None, None),
        P(("region", "sub")),
        P(("region", "sub")),
        P(("region", "sub"), None, None),
    )
    return jax.shard_map(
        local,
        mesh=mesh,
        in_specs=placed,
        out_specs=(P(("region", "sub"), None), P()),
        check_vma=False,
    )
```

```python
import functools

import jax
import jax.numpy as jnp
from jax import lax
from jax.experimental import pallas as pl
from jax.experimental.pallas import tpu as pltpu
from jax.sharding import PartitionSpec as P

ITERS = 3
B = 128
LOAD = 1024
STORE = 1024
CHUNK = 2048
OWN_GROUP = 16
GHOST_GROUP = 8
SECOND = 128
OWN_AT = 256
COUNTS_AT = 512
VMEM_LIMIT = 16 * 1024 * 1024

VMEM = pltpu.VMEM
SMEM = pltpu.SMEM


def vmem_specs(n):
    return [pl.BlockSpec(memory_space=VMEM)] * n


def smem_specs(n):
    return [pl.BlockSpec(memory_space=SMEM)] * n


def in_hbm(x):
    return pltpu.with_memory_space_constraint(x, pltpu.HBM)


def kept(x):
    return pltpu.with_memory_space_constraint(x, VMEM)


def mix(adjoint, state_ref, weight_ref, mixed_ref, rows):
    state = state_ref[rows, :].astype(jnp.float32)
    scaled = ((1.0 - state * state) * adjoint).astype(jnp.bfloat16)
    mixed_ref[rows, :] = lax.dot_general(
        scaled, weight_ref[...], (((1,), (1,)), ((), ())), preferred_element_type=jnp.float32
    ).astype(jnp.bfloat16)


def chunks(row_count):
    def over(body):
        @pl.loop(0, row_count // CHUNK)
        def _(i):
            body(pl.ds(pl.multiple_of(i * CHUNK, CHUNK), CHUNK))

    return over


def add_tiles(plan_ref, begin, groups, size, tiles_ref, mixed_ref, total_ref, base):
    def rows_of(entry):
        return mixed_ref[pl.ds(pl.multiple_of(((entry >> 8) & 255) * B, B), B), :]

    def group(g, carry):
        parts = []
        for u in range(size):
            first = plan_ref[begin + g * size + u]
            second = plan_ref[begin + SECOND + g * size + u]
            col = pl.multiple_of((first >> 16) * B - base, B)
            part = lax.dot_general(
                jnp.concatenate([tiles_ref[first & 255], tiles_ref[second & 255]], axis=0),
                jnp.concatenate([rows_of(first), rows_of(second)], axis=0),
                (((0,), (0,)), ((), ())),
                preferred_element_type=jnp.float32,
            )
            parts.append((col, part))
        for col, part in parts:
            total_ref[pl.ds(col, B), :] += part
        return carry

    lax.fori_loop(0, groups, group, 0)


def ghosts(plan_ref, slots_ref, tiles_ref, mixed_ref, ghost_ref, out_refs, own_blocks):
    ghost_ref[...] = jnp.zeros_like(ghost_ref)
    add_tiles(
        plan_ref, 0, plan_ref[COUNTS_AT], GHOST_GROUP, tiles_ref, mixed_ref, ghost_ref, own_blocks * B
    )
    size = out_refs[0].shape[0]
    for slot, out_ref in enumerate(out_refs):
        at = pl.multiple_of(slots_ref[slot] * size, size)
        out_ref[...] = ghost_ref[pl.ds(at, size), :]


def gather_incoming(in_refs, incoming_ref):
    size = in_refs[0].shape[0]
    for slot, in_ref in enumerate(in_refs):
        incoming_ref[slot * size:(slot + 1) * size, :] = in_ref[...].astype(jnp.bfloat16)


def first_kernel(
    own_blocks, slots_ref, rows_hbm, cols_hbm, targets_hbm, weight_hbm, state_hbm, grad_hbm, tiles_hbm,
    weight_ref, state_ref, grad_ref, tiles_ref, mixed_ref, route_ref, plan_ref, g0, g1, g2, g3,
    rows_ref, cols_ref, waiting_ref, targets_ref, ghost_ref, sems,
):
    tile_count = tiles_hbm.shape[0]
    row_count = grad_hbm.shape[0]
    size = targets_hbm.shape[1]
    ghost_blocks = targets_hbm.shape[0] * size // B
    copies = [
        pltpu.make_async_copy(rows_hbm, rows_ref, sems.at[0]),
        pltpu.make_async_copy(cols_hbm, cols_ref, sems.at[1]),
        pltpu.make_async_copy(targets_hbm, targets_ref, sems.at[2]),
        pltpu.make_async_copy(weight_hbm, weight_ref, sems.at[3]),
    ]
    parts = row_count // LOAD
    for p in range(parts):
        at = pl.ds(p * LOAD, LOAD)
        copies.append(pltpu.make_async_copy(state_hbm.at[at], state_ref.at[at], sems.at[4 + 2 * p]))
        copies.append(pltpu.make_async_copy(grad_hbm.at[at], grad_ref.at[at], sems.at[5 + 2 * p]))
    tile_parts = 4
    some = tile_count // tile_parts
    for q in range(tile_parts):
        at = pl.ds(q * some, some)
        copies.append(
            pltpu.make_async_copy(tiles_hbm.at[at], tiles_ref.at[at], sems.at[4 + 2 * parts + q])
        )
    for copy in copies:
        copy.start()
    tiles_ref[tile_count] = jnp.zeros((B, B), jnp.bfloat16)
    for c in range(own_blocks + ghost_blocks):
        waiting_ref[c] = -1
    for copy in copies[:3]:
        copy.wait()

    steps = tile_count // 3
    band = row_count // steps

    agent = lax.broadcasted_iota(jnp.int32, (band, size), 0)
    target_rows = [targets_ref[pl.ds(slots_ref[4 + slot], 1), :] for slot in range(4)]

    def place(g, counts):
        ghost_count, own_count = counts
        cols = [cols_ref[g * 3 + u] for u in range(3)]
        entries = [rows_ref[g * 3 + u] * 256 + (g * 3 + u) for u in range(3)]
        others = [waiting_ref[col] for col in cols]
        lefts = []
        for u in range(3):
            for v in range(u):
                others[u] = jnp.where(cols[u] == cols[v], lefts[v], others[u])
            lefts.append(jnp.where(others[u] >= 0, -1, entries[u]))
        for u in range(3):
            paired = (others[u] >= 0).astype(jnp.int32)
            is_ghost = (cols[u] >= own_blocks).astype(jnp.int32)
            at = jnp.where(is_ghost == 1, ghost_count, OWN_AT + own_count)
            plan_ref[at] = entries[u] + cols[u] * 65536
            plan_ref[at + SECOND] = others[u]
            ghost_count = ghost_count + is_ghost * paired
            own_count = own_count + (1 - is_ghost) * paired
        for u in range(3):
            waiting_ref[cols[u]] = lefts[u]
        rows = pl.ds(pl.multiple_of(g * band, band), band)
        for slot in range(4):
            route_ref[rows, slot * size:(slot + 1) * size] = jnp.where(
                agent == target_rows[slot] - g * band, 1.0, 0.0
            ).astype(jnp.bfloat16)
        return ghost_count, own_count

    counts = lax.fori_loop(0, steps, place, (jnp.int32(0), jnp.int32(0)))

    def close(begin, blocks, count, group):
        for c in blocks:
            other = waiting_ref[c]
            plan_ref[begin + count] = other + c * 65536
            plan_ref[begin + count + SECOND] = tile_count
            count = count + (other >= 0).astype(jnp.int32)
        for u in range(group):
            plan_ref[begin + count + u] = tile_count + blocks[0] * 65536
            plan_ref[begin + count + u + SECOND] = tile_count
        return (count + group - 1) // group

    all_blocks = list(range(own_blocks + ghost_blocks))
    plan_ref[COUNTS_AT] = close(0, all_blocks[own_blocks:], counts[0], GHOST_GROUP)
    plan_ref[COUNTS_AT + 1] = close(OWN_AT, all_blocks[:own_blocks], counts[1], OWN_GROUP)

    copies[3].wait()
    for p in range(parts):
        copies[4 + 2 * p].wait()
        copies[5 + 2 * p].wait()
        at = pl.ds(p * LOAD, LOAD)
        mix(grad_ref[at, :], state_ref, weight_ref, mixed_ref, at)
    for copy in copies[-tile_parts:]:
        copy.wait()
    ghosts(plan_ref, slots_ref, tiles_ref, mixed_ref, ghost_ref, (g0, g1, g2, g3), own_blocks)


def first_own_kernel(plan_ref, tiles_ref, mixed_ref, grad_ref, out_ref):
    out_ref[...] = grad_ref[...]
    add_tiles(
        plan_ref, OWN_AT, plan_ref[COUNTS_AT + 1], OWN_GROUP, tiles_ref, mixed_ref, out_ref, 0
    )


def own_kernel(plan_ref, tiles_ref, mixed_ref, grad_ref, now_ref, before_ref, out_ref, change_ref):
    change_ref[...] = jnp.zeros_like(change_ref)
    over = chunks(now_ref.shape[0])

    @over
    def _(rows):
        change_ref[...] += squares(now_ref[rows, :] - before_ref[rows, :])

    out_ref[...] = grad_ref[...]
    add_tiles(
        plan_ref, OWN_AT, plan_ref[COUNTS_AT + 1], OWN_GROUP, tiles_ref, mixed_ref, out_ref, 0
    )


def squares(moved):
    total = jnp.sum((moved * moved).reshape(-1, 8, moved.shape[1]), axis=0)
    return total[:, :128] + total[:, 128:]


def middle_kernel(
    own_blocks, slots_ref, plan_ref, weight_ref, state_ref, tiles_ref, route_ref, i0, i1, i2, i3,
    partial_ref, adjoint_ref, mixed_ref, g0, g1, g2, g3, incoming_ref, ghost_ref,
):
    gather_incoming((i0, i1, i2, i3), incoming_ref)
    over = chunks(adjoint_ref.shape[0])

    @over
    def _(rows):
        adjoint = partial_ref[rows, :] + jnp.dot(
            route_ref[rows, :], incoming_ref[...], preferred_element_type=jnp.float32
        )
        adjoint_ref[rows, :] = adjoint
        mix(adjoint, state_ref, weight_ref, mixed_ref, rows)

    ghosts(plan_ref, slots_ref, tiles_ref, mixed_ref, ghost_ref, (g0, g1, g2, g3), own_blocks)


def last_kernel(
    route_ref, i0, i1, i2, i3, before_ref, change0_ref, change1_ref, partial_ref,
    adjoint_hbm, sums_ref, incoming_ref, adjoint_ref, change_ref, sems,
):
    gather_incoming((i0, i1, i2, i3), incoming_ref)
    row_count = partial_ref.shape[0]
    change_ref[...] = jnp.zeros_like(change_ref)

    def store(i):
        rows = pl.ds(pl.multiple_of(i * STORE, STORE), STORE)
        return pltpu.make_async_copy(adjoint_ref.at[rows], adjoint_hbm.at[rows], sems.at[i])

    @pl.loop(0, row_count // STORE)
    def _(i):
        rows = pl.ds(pl.multiple_of(i * STORE, STORE), STORE)
        adjoint = partial_ref[rows, :] + jnp.dot(
            route_ref[rows, :], incoming_ref[...], preferred_element_type=jnp.float32
        )
        adjoint_ref[rows, :] = adjoint
        store(i).start()
        change_ref[...] += squares(adjoint - before_ref[rows, :])

    lane = lax.broadcasted_iota(jnp.int32, sums_ref.shape, 1)
    sums = jnp.zeros(sums_ref.shape, jnp.float32)
    for i, value in enumerate((change0_ref[...], change1_ref[...], change_ref[...])):
        sums = jnp.where(lane == i, jnp.sum(value), sums)
    sums_ref[...] = sums
    for i in range(row_count // STORE):
        store(i).wait()


def local(state, grad_out, weight, tiles, tile_row, tile_col, send_rows):
    row_count, feature_count = state.shape
    own_blocks = row_count // B
    region_count = lax.axis_size("region")
    sub_count = lax.axis_size("sub")
    tile_count = tiles.shape[0]
    ghost_count = send_rows.shape[2]
    ghost_rows = send_rows.shape[1] * ghost_count
    f32, bf16, i32 = jnp.float32, jnp.bfloat16, jnp.int32

    region_odd = lax.axis_index("region") % 2
    sub_odd = lax.axis_index("sub") % 2
    slots = jnp.stack(
        [1 - region_odd, region_odd, 3 - sub_odd, 2 + sub_odd,
         region_odd, 1 - region_odd, 2 + sub_odd, 3 - sub_odd]
    ).astype(i32)

    def swap(value, axis, count, odd):
        partner = [(((i + odd) ^ 1) - odd) % count for i in range(count)]
        return lax.ppermute(value, axis, list(enumerate(partner)))

    def exchange(outgoing):
        return (
            swap(outgoing[0], "region", region_count, 1),
            swap(outgoing[1], "region", region_count, 0),
            swap(outgoing[2], "sub", sub_count, 1),
            swap(outgoing[3], "sub", sub_count, 0),
        )

    params = pltpu.CompilerParams(vmem_limit_bytes=VMEM_LIMIT)
    beside = pl.CostEstimate(flops=10_000_000_000, bytes_accessed=16_000_000, transcendentals=0)
    parts = row_count // LOAD
    agents_f32 = VMEM((row_count, feature_count), f32)
    agents_bf16 = VMEM((row_count, feature_count), bf16)
    outgoing_shapes = (VMEM((ghost_count, feature_count), f32),) * 4
    incoming_scratch = VMEM((ghost_rows, feature_count), bf16)
    ghost_scratch = VMEM((ghost_rows, feature_count), f32)

    targets = send_rows.reshape(4, ghost_count)
    weight_k, state_k, grad_k, tiles_k, mixed, route, plan, *outgoing = pl.pallas_call(
        functools.partial(first_kernel, own_blocks),
        in_specs=smem_specs(1) + [pl.BlockSpec(memory_space=pltpu.HBM)] * 7,
        out_specs=tuple(vmem_specs(6) + smem_specs(1) + vmem_specs(4)),
        out_shape=(
            VMEM(weight.shape, bf16),
            agents_bf16,
            agents_f32,
            VMEM((tile_count + 1, B, B), bf16),
            agents_bf16,
            VMEM((row_count, ghost_rows), bf16),
            jax.ShapeDtypeStruct((COUNTS_AT + 128,), i32),
        )
        + outgoing_shapes,
        scratch_shapes=[
            SMEM((tile_count,), i32),
            SMEM((tile_count,), i32),
            SMEM((128,), i32),
            VMEM((4, ghost_count), i32),
            ghost_scratch,
            pltpu.SemaphoreType.DMA((8 + 2 * parts,)),
        ],
        compiler_params=params,
        name="first",
    )(slots, *[in_hbm(v) for v in (tile_row, tile_col, targets, weight, state, grad_out, tiles)])
    weight_k, state_k, grad_k, tiles_k, route = [
        kept(v) for v in (weight_k, state_k, grad_k, tiles_k, route)
    ]

    before = None
    adjoint = grad_k
    changes = []
    for step in range(ITERS):
        incoming = [kept(v) for v in exchange(outgoing)]
        if step == 0:
            (partial,) = pl.pallas_call(
                first_own_kernel,
                in_specs=smem_specs(1) + vmem_specs(3),
                out_specs=tuple(vmem_specs(1)),
                out_shape=(agents_f32,),
                compiler_params=params,
                cost_estimate=beside,
                name="first_own",
            )(plan, tiles_k, kept(mixed), grad_k)
        else:
            partial, moved = pl.pallas_call(
                own_kernel,
                in_specs=smem_specs(1) + vmem_specs(5),
                out_specs=tuple(vmem_specs(2)),
                out_shape=(agents_f32, VMEM((8, 128), f32)),
                compiler_params=params,
                cost_estimate=beside,
                name="own",
            )(plan, tiles_k, kept(mixed), grad_k, kept(adjoint), kept(before))
            changes.append(kept(moved))
        before = adjoint
        if step < ITERS - 1:
            adjoint, mixed, *outgoing = pl.pallas_call(
                functools.partial(middle_kernel, own_blocks),
                in_specs=smem_specs(2) + vmem_specs(9),
                out_specs=tuple(vmem_specs(6)),
                out_shape=(agents_f32, agents_bf16) + outgoing_shapes,
                scratch_shapes=[incoming_scratch, ghost_scratch],
                input_output_aliases={10: 0},
                compiler_params=params,
                name="middle",
            )(slots, plan, weight_k, state_k, tiles_k, route, *incoming, kept(partial))
        else:
            adjoint, sums = pl.pallas_call(
                last_kernel,
                in_specs=vmem_specs(9),
                out_specs=(pl.BlockSpec(memory_space=pltpu.HBM), pl.BlockSpec(memory_space=VMEM)),
                out_shape=(
                    pltpu.HBM((row_count, feature_count), f32),
                    VMEM((region_count * sub_count, 128), f32),
                ),
                scratch_shapes=[
                    incoming_scratch,
                    agents_f32,
                    VMEM((8, 128), f32),
                    pltpu.SemaphoreType.DMA((row_count // STORE,)),
                ],
                compiler_params=params,
                name="last",
            )(route, *incoming, kept(before), *changes, kept(partial))

    sums = lax.all_to_all(sums, ("region", "sub"), 0, 0, tiled=True)
    total = jnp.sum(sums, axis=0)
    inverse_count = 1.0 / (region_count * sub_count * row_count * feature_count)
    residual_norms = jnp.sqrt(total[:ITERS] * inverse_count + 1e-06)
    return adjoint, residual_norms


def solution(mesh):
    placed = (
        P(("region", "sub"), None),
        P(("region", "sub"), None),
        P(),
        P(("region", "sub"), None, None),
        P(("region", "sub")),
        P(("region", "sub")),
        P(("region", "sub"), None, None),
    )
    return jax.shard_map(
        local,
        mesh=mesh,
        in_specs=placed,
        out_specs=(P(("region", "sub"), None), P()),
        check_vma=False,
    )
```

```python
import functools

import jax
import jax.numpy as jnp
from jax import lax
from jax.experimental import pallas as pl
from jax.experimental.pallas import tpu as pltpu
from jax.sharding import PartitionSpec as P

ITERS = 3
B = 128
LOAD = 1024
STORE = 1024
CHUNK = 2048
OWN_GROUP = 16
GHOST_GROUP = 12
SECOND = 128
OWN_AT = 256
COUNTS_AT = 512
VMEM_LIMIT = 16 * 1024 * 1024

VMEM = pltpu.VMEM
SMEM = pltpu.SMEM


def vmem_specs(n):
    return [pl.BlockSpec(memory_space=VMEM)] * n


def smem_specs(n):
    return [pl.BlockSpec(memory_space=SMEM)] * n


def in_hbm(x):
    return pltpu.with_memory_space_constraint(x, pltpu.HBM)


def kept(x):
    return pltpu.with_memory_space_constraint(x, VMEM)


def mix(adjoint, state_ref, weight_ref, mixed_ref, rows):
    state = state_ref[rows, :].astype(jnp.float32)
    scaled = ((1.0 - state * state) * adjoint).astype(jnp.bfloat16)
    mixed_ref[rows, :] = lax.dot_general(
        scaled, weight_ref[...], (((1,), (1,)), ((), ())), preferred_element_type=jnp.float32
    ).astype(jnp.bfloat16)


def chunks(row_count):
    def over(body):
        @pl.loop(0, row_count // CHUNK)
        def _(i):
            body(pl.ds(pl.multiple_of(i * CHUNK, CHUNK), CHUNK))

    return over


def add_tiles(plan_ref, begin, groups, size, tiles_ref, mixed_ref, total_ref, base):
    def rows_of(entry):
        return mixed_ref[pl.ds(pl.multiple_of(((entry >> 8) & 255) * B, B), B), :]

    def group(g, carry):
        parts = []
        for u in range(size):
            first = plan_ref[begin + g * size + u]
            second = plan_ref[begin + SECOND + g * size + u]
            col = pl.multiple_of((first >> 16) * B - base, B)
            part = lax.dot_general(
                jnp.concatenate([tiles_ref[first & 255], tiles_ref[second & 255]], axis=0),
                jnp.concatenate([rows_of(first), rows_of(second)], axis=0),
                (((0,), (0,)), ((), ())),
                preferred_element_type=jnp.float32,
            )
            parts.append((col, part))
        for col, part in parts:
            total_ref[pl.ds(col, B), :] += part
        return carry

    lax.fori_loop(0, groups, group, 0)


def ghosts(plan_ref, slots_ref, tiles_ref, mixed_ref, ghost_ref, out_refs, own_blocks):
    ghost_ref[...] = jnp.zeros_like(ghost_ref)
    add_tiles(
        plan_ref, 0, plan_ref[COUNTS_AT], GHOST_GROUP, tiles_ref, mixed_ref, ghost_ref, own_blocks * B
    )
    size = out_refs[0].shape[0]
    for slot, out_ref in enumerate(out_refs):
        at = pl.multiple_of(slots_ref[slot] * size, size)
        out_ref[...] = ghost_ref[pl.ds(at, size), :]


def gather_incoming(in_refs, incoming_ref):
    size = in_refs[0].shape[0]
    for slot, in_ref in enumerate(in_refs):
        incoming_ref[slot * size:(slot + 1) * size, :] = in_ref[...].astype(jnp.bfloat16)


def first_kernel(
    own_blocks, slots_ref, rows_hbm, cols_hbm, targets_hbm, weight_hbm, state_hbm, grad_hbm, tiles_hbm,
    weight_ref, state_ref, grad_ref, tiles_ref, mixed_ref, route_ref, plan_ref, g0, g1, g2, g3,
    rows_ref, cols_ref, waiting_ref, targets_ref, ghost_ref, sems,
):
    tile_count = tiles_hbm.shape[0]
    row_count = grad_hbm.shape[0]
    size = targets_hbm.shape[1]
    ghost_blocks = targets_hbm.shape[0] * size // B
    copies = [
        pltpu.make_async_copy(rows_hbm, rows_ref, sems.at[0]),
        pltpu.make_async_copy(cols_hbm, cols_ref, sems.at[1]),
        pltpu.make_async_copy(targets_hbm, targets_ref, sems.at[2]),
        pltpu.make_async_copy(weight_hbm, weight_ref, sems.at[3]),
    ]
    parts = row_count // LOAD
    for p in range(parts):
        at = pl.ds(p * LOAD, LOAD)
        copies.append(pltpu.make_async_copy(state_hbm.at[at], state_ref.at[at], sems.at[4 + 2 * p]))
        copies.append(pltpu.make_async_copy(grad_hbm.at[at], grad_ref.at[at], sems.at[5 + 2 * p]))
    tile_parts = 4
    some = tile_count // tile_parts
    for q in range(tile_parts):
        at = pl.ds(q * some, some)
        copies.append(
            pltpu.make_async_copy(tiles_hbm.at[at], tiles_ref.at[at], sems.at[4 + 2 * parts + q])
        )
    for copy in copies:
        copy.start()
    tiles_ref[tile_count] = jnp.zeros((B, B), jnp.bfloat16)
    for c in range(own_blocks + ghost_blocks):
        waiting_ref[c] = -1
    for copy in copies[:3]:
        copy.wait()

    steps = tile_count // 3
    band = row_count // steps

    agent = lax.broadcasted_iota(jnp.int32, (band, size), 0)
    target_rows = [targets_ref[pl.ds(slots_ref[4 + slot], 1), :] for slot in range(4)]

    def place(g, counts):
        ghost_count, own_count = counts
        cols = [cols_ref[g * 3 + u] for u in range(3)]
        entries = [rows_ref[g * 3 + u] * 256 + (g * 3 + u) for u in range(3)]
        others = [waiting_ref[col] for col in cols]
        lefts = []
        for u in range(3):
            for v in range(u):
                others[u] = jnp.where(cols[u] == cols[v], lefts[v], others[u])
            lefts.append(jnp.where(others[u] >= 0, -1, entries[u]))
        for u in range(3):
            paired = (others[u] >= 0).astype(jnp.int32)
            is_ghost = (cols[u] >= own_blocks).astype(jnp.int32)
            at = jnp.where(is_ghost == 1, ghost_count, OWN_AT + own_count)
            plan_ref[at] = entries[u] + cols[u] * 65536
            plan_ref[at + SECOND] = others[u]
            ghost_count = ghost_count + is_ghost * paired
            own_count = own_count + (1 - is_ghost) * paired
        for u in range(3):
            waiting_ref[cols[u]] = lefts[u]
        rows = pl.ds(pl.multiple_of(g * band, band), band)
        for slot in range(4):
            route_ref[rows, slot * size:(slot + 1) * size] = jnp.where(
                agent == target_rows[slot] - g * band, 1.0, 0.0
            ).astype(jnp.bfloat16)
        return ghost_count, own_count

    counts = lax.fori_loop(0, steps, place, (jnp.int32(0), jnp.int32(0)))

    def close(begin, blocks, count, group):
        for c in blocks:
            other = waiting_ref[c]
            plan_ref[begin + count] = other + c * 65536
            plan_ref[begin + count + SECOND] = tile_count
            count = count + (other >= 0).astype(jnp.int32)
        for u in range(group):
            plan_ref[begin + count + u] = tile_count + blocks[0] * 65536
            plan_ref[begin + count + u + SECOND] = tile_count
        return (count + group - 1) // group

    all_blocks = list(range(own_blocks + ghost_blocks))
    plan_ref[COUNTS_AT] = close(0, all_blocks[own_blocks:], counts[0], GHOST_GROUP)
    plan_ref[COUNTS_AT + 1] = close(OWN_AT, all_blocks[:own_blocks], counts[1], OWN_GROUP)

    copies[3].wait()
    for p in range(parts):
        copies[4 + 2 * p].wait()
        copies[5 + 2 * p].wait()
        at = pl.ds(p * LOAD, LOAD)
        mix(grad_ref[at, :], state_ref, weight_ref, mixed_ref, at)
    for copy in copies[-tile_parts:]:
        copy.wait()
    ghosts(plan_ref, slots_ref, tiles_ref, mixed_ref, ghost_ref, (g0, g1, g2, g3), own_blocks)


def first_own_kernel(plan_ref, tiles_ref, mixed_ref, grad_ref, out_ref):
    out_ref[...] = grad_ref[...]
    add_tiles(
        plan_ref, OWN_AT, plan_ref[COUNTS_AT + 1], OWN_GROUP, tiles_ref, mixed_ref, out_ref, 0
    )


def own_kernel(plan_ref, tiles_ref, mixed_ref, grad_ref, now_ref, before_ref, out_ref, change_ref):
    change_ref[...] = jnp.zeros_like(change_ref)
    over = chunks(now_ref.shape[0])

    @over
    def _(rows):
        change_ref[...] += squares(now_ref[rows, :] - before_ref[rows, :])

    out_ref[...] = grad_ref[...]
    add_tiles(
        plan_ref, OWN_AT, plan_ref[COUNTS_AT + 1], OWN_GROUP, tiles_ref, mixed_ref, out_ref, 0
    )


def squares(moved):
    total = jnp.sum((moved * moved).reshape(-1, 8, moved.shape[1]), axis=0)
    return total[:, :128] + total[:, 128:]


def middle_kernel(
    own_blocks, slots_ref, plan_ref, weight_ref, state_ref, tiles_ref, route_ref, i0, i1, i2, i3,
    partial_ref, adjoint_ref, mixed_ref, g0, g1, g2, g3, incoming_ref, ghost_ref,
):
    gather_incoming((i0, i1, i2, i3), incoming_ref)
    over = chunks(adjoint_ref.shape[0])

    @over
    def _(rows):
        adjoint = partial_ref[rows, :] + jnp.dot(
            route_ref[rows, :], incoming_ref[...], preferred_element_type=jnp.float32
        )
        adjoint_ref[rows, :] = adjoint
        mix(adjoint, state_ref, weight_ref, mixed_ref, rows)

    ghosts(plan_ref, slots_ref, tiles_ref, mixed_ref, ghost_ref, (g0, g1, g2, g3), own_blocks)


def last_kernel(
    route_ref, i0, i1, i2, i3, before_ref, change0_ref, change1_ref, partial_ref,
    adjoint_hbm, sums_ref, incoming_ref, adjoint_ref, change_ref, sems,
):
    gather_incoming((i0, i1, i2, i3), incoming_ref)
    row_count = partial_ref.shape[0]
    change_ref[...] = jnp.zeros_like(change_ref)

    def store(i):
        rows = pl.ds(pl.multiple_of(i * STORE, STORE), STORE)
        return pltpu.make_async_copy(adjoint_ref.at[rows], adjoint_hbm.at[rows], sems.at[i])

    @pl.loop(0, row_count // STORE)
    def _(i):
        rows = pl.ds(pl.multiple_of(i * STORE, STORE), STORE)
        adjoint = partial_ref[rows, :] + jnp.dot(
            route_ref[rows, :], incoming_ref[...], preferred_element_type=jnp.float32
        )
        adjoint_ref[rows, :] = adjoint
        store(i).start()
        change_ref[...] += squares(adjoint - before_ref[rows, :])

    lane = lax.broadcasted_iota(jnp.int32, sums_ref.shape, 1)
    sums = jnp.zeros(sums_ref.shape, jnp.float32)
    for i, value in enumerate((change0_ref[...], change1_ref[...], change_ref[...])):
        sums = jnp.where(lane == i, jnp.sum(value), sums)
    sums_ref[...] = sums
    for i in range(row_count // STORE):
        store(i).wait()


def local(state, grad_out, weight, tiles, tile_row, tile_col, send_rows):
    row_count, feature_count = state.shape
    own_blocks = row_count // B
    region_count = lax.axis_size("region")
    sub_count = lax.axis_size("sub")
    tile_count = tiles.shape[0]
    ghost_count = send_rows.shape[2]
    ghost_rows = send_rows.shape[1] * ghost_count
    f32, bf16, i32 = jnp.float32, jnp.bfloat16, jnp.int32

    region_odd = lax.axis_index("region") % 2
    sub_odd = lax.axis_index("sub") % 2
    slots = jnp.stack(
        [1 - region_odd, region_odd, 3 - sub_odd, 2 + sub_odd,
         region_odd, 1 - region_odd, 2 + sub_odd, 3 - sub_odd]
    ).astype(i32)

    def swap(value, axis, count, odd):
        partner = [(((i + odd) ^ 1) - odd) % count for i in range(count)]
        return lax.ppermute(value, axis, list(enumerate(partner)))

    def exchange(outgoing):
        return (
            swap(outgoing[0], "region", region_count, 1),
            swap(outgoing[1], "region", region_count, 0),
            swap(outgoing[2], "sub", sub_count, 1),
            swap(outgoing[3], "sub", sub_count, 0),
        )

    params = pltpu.CompilerParams(vmem_limit_bytes=VMEM_LIMIT)
    beside = pl.CostEstimate(flops=10_000_000_000, bytes_accessed=16_000_000, transcendentals=0)
    parts = row_count // LOAD
    agents_f32 = VMEM((row_count, feature_count), f32)
    agents_bf16 = VMEM((row_count, feature_count), bf16)
    outgoing_shapes = (VMEM((ghost_count, feature_count), f32),) * 4
    incoming_scratch = VMEM((ghost_rows, feature_count), bf16)
    ghost_scratch = VMEM((ghost_rows, feature_count), f32)

    targets = send_rows.reshape(4, ghost_count)
    weight_k, state_k, grad_k, tiles_k, mixed, route, plan, *outgoing = pl.pallas_call(
        functools.partial(first_kernel, own_blocks),
        in_specs=smem_specs(1) + [pl.BlockSpec(memory_space=pltpu.HBM)] * 7,
        out_specs=tuple(vmem_specs(6) + smem_specs(1) + vmem_specs(4)),
        out_shape=(
            VMEM(weight.shape, bf16),
            agents_bf16,
            agents_f32,
            VMEM((tile_count + 1, B, B), bf16),
            agents_bf16,
            VMEM((row_count, ghost_rows), bf16),
            jax.ShapeDtypeStruct((COUNTS_AT + 128,), i32),
        )
        + outgoing_shapes,
        scratch_shapes=[
            SMEM((tile_count,), i32),
            SMEM((tile_count,), i32),
            SMEM((128,), i32),
            VMEM((4, ghost_count), i32),
            ghost_scratch,
            pltpu.SemaphoreType.DMA((8 + 2 * parts,)),
        ],
        compiler_params=params,
        name="first",
    )(slots, *[in_hbm(v) for v in (tile_row, tile_col, targets, weight, state, grad_out, tiles)])
    weight_k, state_k, grad_k, tiles_k, route = [
        kept(v) for v in (weight_k, state_k, grad_k, tiles_k, route)
    ]

    before = None
    adjoint = grad_k
    changes = []
    for step in range(ITERS):
        incoming = [kept(v) for v in exchange(outgoing)]
        if step == 0:
            (partial,) = pl.pallas_call(
                first_own_kernel,
                in_specs=smem_specs(1) + vmem_specs(3),
                out_specs=tuple(vmem_specs(1)),
                out_shape=(agents_f32,),
                compiler_params=params,
                cost_estimate=beside,
                name="first_own",
            )(plan, tiles_k, kept(mixed), grad_k)
        else:
            partial, moved = pl.pallas_call(
                own_kernel,
                in_specs=smem_specs(1) + vmem_specs(5),
                out_specs=tuple(vmem_specs(2)),
                out_shape=(agents_f32, VMEM((8, 128), f32)),
                compiler_params=params,
                cost_estimate=beside,
                name="own",
            )(plan, tiles_k, kept(mixed), grad_k, kept(adjoint), kept(before))
            changes.append(kept(moved))
        before = adjoint
        if step < ITERS - 1:
            adjoint, mixed, *outgoing = pl.pallas_call(
                functools.partial(middle_kernel, own_blocks),
                in_specs=smem_specs(2) + vmem_specs(9),
                out_specs=tuple(vmem_specs(6)),
                out_shape=(agents_f32, agents_bf16) + outgoing_shapes,
                scratch_shapes=[incoming_scratch, ghost_scratch],
                input_output_aliases={10: 0},
                compiler_params=params,
                name="middle",
            )(slots, plan, weight_k, state_k, tiles_k, route, *incoming, kept(partial))
        else:
            adjoint, sums = pl.pallas_call(
                last_kernel,
                in_specs=vmem_specs(9),
                out_specs=(pl.BlockSpec(memory_space=pltpu.HBM), pl.BlockSpec(memory_space=VMEM)),
                out_shape=(
                    pltpu.HBM((row_count, feature_count), f32),
                    VMEM((region_count * sub_count, 128), f32),
                ),
                scratch_shapes=[
                    incoming_scratch,
                    agents_f32,
                    VMEM((8, 128), f32),
                    pltpu.SemaphoreType.DMA((row_count // STORE,)),
                ],
                compiler_params=params,
                name="last",
            )(route, *incoming, kept(before), *changes, kept(partial))

    sums = lax.all_to_all(sums, ("region", "sub"), 0, 0, tiled=True)
    total = jnp.sum(sums, axis=0)
    inverse_count = 1.0 / (region_count * sub_count * row_count * feature_count)
    residual_norms = jnp.sqrt(total[:ITERS] * inverse_count + 1e-06)
    return adjoint, residual_norms


def solution(mesh):
    placed = (
        P(("region", "sub"), None),
        P(("region", "sub"), None),
        P(),
        P(("region", "sub"), None, None),
        P(("region", "sub")),
        P(("region", "sub")),
        P(("region", "sub"), None, None),
    )
    return jax.shard_map(
        local,
        mesh=mesh,
        in_specs=placed,
        out_specs=(P(("region", "sub"), None), P()),
        check_vma=False,
    )
```

```python
import functools

import jax
import jax.numpy as jnp
from jax import lax
from jax.experimental import pallas as pl
from jax.experimental.pallas import tpu as pltpu
from jax.sharding import PartitionSpec as P

ITERS = 3
B = 128
LOAD = 1024
STORE = 1024
CHUNK = 2048
OWN_GROUP = 16
GHOST_GROUP = 12
SECOND = 128
OWN_AT = 256
COUNTS_AT = 512
VMEM_LIMIT = 16 * 1024 * 1024

VMEM = pltpu.VMEM
SMEM = pltpu.SMEM


def vmem_specs(n):
    return [pl.BlockSpec(memory_space=VMEM)] * n


def smem_specs(n):
    return [pl.BlockSpec(memory_space=SMEM)] * n


def in_hbm(x):
    return pltpu.with_memory_space_constraint(x, pltpu.HBM)


def kept(x):
    return pltpu.with_memory_space_constraint(x, VMEM)


def mix(adjoint, state_ref, weight_ref, mixed_ref, rows):
    state = state_ref[rows, :].astype(jnp.float32)
    scaled = ((1.0 - state * state) * adjoint).astype(jnp.bfloat16)
    mixed_ref[rows, :] = lax.dot_general(
        scaled, weight_ref[...], (((1,), (1,)), ((), ())), preferred_element_type=jnp.float32
    ).astype(jnp.bfloat16)


def chunks(row_count):
    def over(body):
        @pl.loop(0, row_count // CHUNK)
        def _(i):
            body(pl.ds(pl.multiple_of(i * CHUNK, CHUNK), CHUNK))

    return over


def add_tiles(plan_ref, begin, groups, size, tiles_ref, mixed_ref, total_ref, base):
    def rows_of(entry):
        return mixed_ref[pl.ds(pl.multiple_of(((entry >> 8) & 255) * B, B), B), :]

    def group(g, carry):
        parts = []
        for u in range(size):
            first = plan_ref[begin + g * size + u]
            second = plan_ref[begin + SECOND + g * size + u]
            col = pl.multiple_of((first >> 16) * B - base, B)
            part = lax.dot_general(
                jnp.concatenate([tiles_ref[first & 255], tiles_ref[second & 255]], axis=0),
                jnp.concatenate([rows_of(first), rows_of(second)], axis=0),
                (((0,), (0,)), ((), ())),
                preferred_element_type=jnp.float32,
            )
            parts.append((col, part))
        for col, part in parts:
            total_ref[pl.ds(col, B), :] += part
        return carry

    lax.fori_loop(0, groups, group, 0)


def ghosts(plan_ref, slots_ref, tiles_ref, mixed_ref, ghost_ref, out_refs, own_blocks):
    ghost_ref[...] = jnp.zeros_like(ghost_ref)
    add_tiles(
        plan_ref, 0, plan_ref[COUNTS_AT], GHOST_GROUP, tiles_ref, mixed_ref, ghost_ref, own_blocks * B
    )
    size = out_refs[0].shape[0]
    for slot, out_ref in enumerate(out_refs):
        at = pl.multiple_of(slots_ref[slot] * size, size)
        out_ref[...] = ghost_ref[pl.ds(at, size), :]


def gather_incoming(in_refs, incoming_ref):
    size = in_refs[0].shape[0]
    for slot, in_ref in enumerate(in_refs):
        incoming_ref[slot * size:(slot + 1) * size, :] = in_ref[...].astype(jnp.bfloat16)


def first_kernel(
    own_blocks, slots_ref, rows_hbm, cols_hbm, targets_hbm, weight_hbm, state_hbm, grad_hbm, tiles_hbm,
    weight_ref, state_ref, grad_ref, tiles_ref, mixed_ref, route_ref, plan_ref, g0, g1, g2, g3,
    rows_ref, cols_ref, waiting_ref, targets_ref, ghost_ref, sems,
):
    tile_count = tiles_hbm.shape[0]
    row_count = grad_hbm.shape[0]
    size = targets_hbm.shape[1]
    ghost_blocks = targets_hbm.shape[0] * size // B
    copies = [
        pltpu.make_async_copy(rows_hbm, rows_ref, sems.at[0]),
        pltpu.make_async_copy(cols_hbm, cols_ref, sems.at[1]),
        pltpu.make_async_copy(targets_hbm, targets_ref, sems.at[2]),
        pltpu.make_async_copy(weight_hbm, weight_ref, sems.at[3]),
    ]
    parts = row_count // LOAD
    for p in range(parts):
        at = pl.ds(p * LOAD, LOAD)
        copies.append(pltpu.make_async_copy(state_hbm.at[at], state_ref.at[at], sems.at[4 + 2 * p]))
        copies.append(pltpu.make_async_copy(grad_hbm.at[at], grad_ref.at[at], sems.at[5 + 2 * p]))
    tile_parts = 4
    some = tile_count // tile_parts
    for q in range(tile_parts):
        at = pl.ds(q * some, some)
        copies.append(
            pltpu.make_async_copy(tiles_hbm.at[at], tiles_ref.at[at], sems.at[4 + 2 * parts + q])
        )
    for copy in copies:
        copy.start()
    tiles_ref[tile_count] = jnp.zeros((B, B), jnp.bfloat16)
    for c in range(own_blocks + ghost_blocks):
        waiting_ref[c] = -1
    for copy in copies[:3]:
        copy.wait()

    steps = tile_count // 6
    band = row_count // steps

    agent = lax.broadcasted_iota(jnp.int32, (band, size), 0)
    target_rows = [targets_ref[pl.ds(slots_ref[4 + slot], 1), :] for slot in range(4)]

    def place(g, counts):
        ghost_count, own_count = counts
        cols = [cols_ref[g * 6 + u] for u in range(6)]
        entries = [rows_ref[g * 6 + u] * 256 + (g * 6 + u) for u in range(6)]
        others = [waiting_ref[col] for col in cols]
        lefts = []
        for u in range(6):
            for v in range(u):
                others[u] = jnp.where(cols[u] == cols[v], lefts[v], others[u])
            lefts.append(jnp.where(others[u] >= 0, -1, entries[u]))
        for u in range(6):
            paired = (others[u] >= 0).astype(jnp.int32)
            is_ghost = (cols[u] >= own_blocks).astype(jnp.int32)
            at = jnp.where(is_ghost == 1, ghost_count, OWN_AT + own_count)
            plan_ref[at] = entries[u] + cols[u] * 65536
            plan_ref[at + SECOND] = others[u]
            ghost_count = ghost_count + is_ghost * paired
            own_count = own_count + (1 - is_ghost) * paired
        for u in range(6):
            waiting_ref[cols[u]] = lefts[u]
        rows = pl.ds(pl.multiple_of(g * band, band), band)
        for slot in range(4):
            route_ref[rows, slot * size:(slot + 1) * size] = jnp.where(
                agent == target_rows[slot] - g * band, 1.0, 0.0
            ).astype(jnp.bfloat16)
        return ghost_count, own_count

    counts = lax.fori_loop(0, steps, place, (jnp.int32(0), jnp.int32(0)))

    def close(begin, blocks, count, group):
        for c in blocks:
            other = waiting_ref[c]
            plan_ref[begin + count] = other + c * 65536
            plan_ref[begin + count + SECOND] = tile_count
            count = count + (other >= 0).astype(jnp.int32)
        for u in range(group):
            plan_ref[begin + count + u] = tile_count + blocks[0] * 65536
            plan_ref[begin + count + u + SECOND] = tile_count
        return (count + group - 1) // group

    all_blocks = list(range(own_blocks + ghost_blocks))
    plan_ref[COUNTS_AT] = close(0, all_blocks[own_blocks:], counts[0], GHOST_GROUP)
    plan_ref[COUNTS_AT + 1] = close(OWN_AT, all_blocks[:own_blocks], counts[1], OWN_GROUP)

    copies[3].wait()
    for p in range(parts):
        copies[4 + 2 * p].wait()
        copies[5 + 2 * p].wait()
        at = pl.ds(p * LOAD, LOAD)
        mix(grad_ref[at, :], state_ref, weight_ref, mixed_ref, at)
    for copy in copies[-tile_parts:]:
        copy.wait()
    ghosts(plan_ref, slots_ref, tiles_ref, mixed_ref, ghost_ref, (g0, g1, g2, g3), own_blocks)


def first_own_kernel(plan_ref, tiles_ref, mixed_ref, grad_ref, out_ref):
    out_ref[...] = grad_ref[...]
    add_tiles(
        plan_ref, OWN_AT, plan_ref[COUNTS_AT + 1], OWN_GROUP, tiles_ref, mixed_ref, out_ref, 0
    )


def own_kernel(plan_ref, tiles_ref, mixed_ref, grad_ref, now_ref, before_ref, out_ref, change_ref):
    change_ref[...] = jnp.zeros_like(change_ref)
    over = chunks(now_ref.shape[0])

    @over
    def _(rows):
        change_ref[...] += squares(now_ref[rows, :] - before_ref[rows, :])

    out_ref[...] = grad_ref[...]
    add_tiles(
        plan_ref, OWN_AT, plan_ref[COUNTS_AT + 1], OWN_GROUP, tiles_ref, mixed_ref, out_ref, 0
    )


def squares(moved):
    total = jnp.sum((moved * moved).reshape(-1, 8, moved.shape[1]), axis=0)
    return total[:, :128] + total[:, 128:]


def middle_kernel(
    own_blocks, slots_ref, plan_ref, weight_ref, state_ref, tiles_ref, route_ref, i0, i1, i2, i3,
    partial_ref, adjoint_ref, mixed_ref, g0, g1, g2, g3, incoming_ref, ghost_ref,
):
    gather_incoming((i0, i1, i2, i3), incoming_ref)
    over = chunks(adjoint_ref.shape[0])

    @over
    def _(rows):
        adjoint = partial_ref[rows, :] + jnp.dot(
            route_ref[rows, :], incoming_ref[...], preferred_element_type=jnp.float32
        )
        adjoint_ref[rows, :] = adjoint
        mix(adjoint, state_ref, weight_ref, mixed_ref, rows)

    ghosts(plan_ref, slots_ref, tiles_ref, mixed_ref, ghost_ref, (g0, g1, g2, g3), own_blocks)


def last_kernel(
    route_ref, i0, i1, i2, i3, before_ref, change0_ref, change1_ref, partial_ref,
    adjoint_hbm, sums_ref, incoming_ref, adjoint_ref, change_ref, sems,
):
    gather_incoming((i0, i1, i2, i3), incoming_ref)
    row_count = partial_ref.shape[0]
    change_ref[...] = jnp.zeros_like(change_ref)

    def store(i):
        rows = pl.ds(pl.multiple_of(i * STORE, STORE), STORE)
        return pltpu.make_async_copy(adjoint_ref.at[rows], adjoint_hbm.at[rows], sems.at[i])

    @pl.loop(0, row_count // STORE)
    def _(i):
        rows = pl.ds(pl.multiple_of(i * STORE, STORE), STORE)
        adjoint = partial_ref[rows, :] + jnp.dot(
            route_ref[rows, :], incoming_ref[...], preferred_element_type=jnp.float32
        )
        adjoint_ref[rows, :] = adjoint
        store(i).start()
        change_ref[...] += squares(adjoint - before_ref[rows, :])

    lane = lax.broadcasted_iota(jnp.int32, sums_ref.shape, 1)
    sums = jnp.zeros(sums_ref.shape, jnp.float32)
    for i, value in enumerate((change0_ref[...], change1_ref[...], change_ref[...])):
        sums = jnp.where(lane == i, jnp.sum(value), sums)
    sums_ref[...] = sums
    for i in range(row_count // STORE):
        store(i).wait()


def local(state, grad_out, weight, tiles, tile_row, tile_col, send_rows):
    row_count, feature_count = state.shape
    own_blocks = row_count // B
    region_count = lax.axis_size("region")
    sub_count = lax.axis_size("sub")
    tile_count = tiles.shape[0]
    ghost_count = send_rows.shape[2]
    ghost_rows = send_rows.shape[1] * ghost_count
    f32, bf16, i32 = jnp.float32, jnp.bfloat16, jnp.int32

    region_odd = lax.axis_index("region") % 2
    sub_odd = lax.axis_index("sub") % 2
    slots = jnp.stack(
        [1 - region_odd, region_odd, 3 - sub_odd, 2 + sub_odd,
         region_odd, 1 - region_odd, 2 + sub_odd, 3 - sub_odd]
    ).astype(i32)

    def swap(value, axis, count, odd):
        partner = [(((i + odd) ^ 1) - odd) % count for i in range(count)]
        return lax.ppermute(value, axis, list(enumerate(partner)))

    def exchange(outgoing):
        return (
            swap(outgoing[0], "region", region_count, 1),
            swap(outgoing[1], "region", region_count, 0),
            swap(outgoing[2], "sub", sub_count, 1),
            swap(outgoing[3], "sub", sub_count, 0),
        )

    params = pltpu.CompilerParams(vmem_limit_bytes=VMEM_LIMIT)
    beside = pl.CostEstimate(flops=10_000_000_000, bytes_accessed=16_000_000, transcendentals=0)
    parts = row_count // LOAD
    agents_f32 = VMEM((row_count, feature_count), f32)
    agents_bf16 = VMEM((row_count, feature_count), bf16)
    outgoing_shapes = (VMEM((ghost_count, feature_count), f32),) * 4
    incoming_scratch = VMEM((ghost_rows, feature_count), bf16)
    ghost_scratch = VMEM((ghost_rows, feature_count), f32)

    targets = send_rows.reshape(4, ghost_count)
    weight_k, state_k, grad_k, tiles_k, mixed, route, plan, *outgoing = pl.pallas_call(
        functools.partial(first_kernel, own_blocks),
        in_specs=smem_specs(1) + [pl.BlockSpec(memory_space=pltpu.HBM)] * 7,
        out_specs=tuple(vmem_specs(6) + smem_specs(1) + vmem_specs(4)),
        out_shape=(
            VMEM(weight.shape, bf16),
            agents_bf16,
            agents_f32,
            VMEM((tile_count + 1, B, B), bf16),
            agents_bf16,
            VMEM((row_count, ghost_rows), bf16),
            jax.ShapeDtypeStruct((COUNTS_AT + 128,), i32),
        )
        + outgoing_shapes,
        scratch_shapes=[
            SMEM((tile_count,), i32),
            SMEM((tile_count,), i32),
            SMEM((128,), i32),
            VMEM((4, ghost_count), i32),
            ghost_scratch,
            pltpu.SemaphoreType.DMA((8 + 2 * parts,)),
        ],
        compiler_params=params,
        name="first",
    )(slots, *[in_hbm(v) for v in (tile_row, tile_col, targets, weight, state, grad_out, tiles)])
    weight_k, state_k, grad_k, tiles_k, route = [
        kept(v) for v in (weight_k, state_k, grad_k, tiles_k, route)
    ]

    before = None
    adjoint = grad_k
    changes = []
    for step in range(ITERS):
        incoming = [kept(v) for v in exchange(outgoing)]
        if step == 0:
            (partial,) = pl.pallas_call(
                first_own_kernel,
                in_specs=smem_specs(1) + vmem_specs(3),
                out_specs=tuple(vmem_specs(1)),
                out_shape=(agents_f32,),
                compiler_params=params,
                cost_estimate=beside,
                name="first_own",
            )(plan, tiles_k, kept(mixed), grad_k)
        else:
            partial, moved = pl.pallas_call(
                own_kernel,
                in_specs=smem_specs(1) + vmem_specs(5),
                out_specs=tuple(vmem_specs(2)),
                out_shape=(agents_f32, VMEM((8, 128), f32)),
                compiler_params=params,
                cost_estimate=beside,
                name="own",
            )(plan, tiles_k, kept(mixed), grad_k, kept(adjoint), kept(before))
            changes.append(kept(moved))
        before = adjoint
        if step < ITERS - 1:
            adjoint, mixed, *outgoing = pl.pallas_call(
                functools.partial(middle_kernel, own_blocks),
                in_specs=smem_specs(2) + vmem_specs(9),
                out_specs=tuple(vmem_specs(6)),
                out_shape=(agents_f32, agents_bf16) + outgoing_shapes,
                scratch_shapes=[incoming_scratch, ghost_scratch],
                input_output_aliases={10: 0},
                compiler_params=params,
                name="middle",
            )(slots, plan, weight_k, state_k, tiles_k, route, *incoming, kept(partial))
        else:
            adjoint, sums = pl.pallas_call(
                last_kernel,
                in_specs=vmem_specs(9),
                out_specs=(pl.BlockSpec(memory_space=pltpu.HBM), pl.BlockSpec(memory_space=VMEM)),
                out_shape=(
                    pltpu.HBM((row_count, feature_count), f32),
                    VMEM((region_count * sub_count, 128), f32),
                ),
                scratch_shapes=[
                    incoming_scratch,
                    agents_f32,
                    VMEM((8, 128), f32),
                    pltpu.SemaphoreType.DMA((row_count // STORE,)),
                ],
                compiler_params=params,
                name="last",
            )(route, *incoming, kept(before), *changes, kept(partial))

    sums = lax.all_to_all(sums, ("region", "sub"), 0, 0, tiled=True)
    total = jnp.sum(sums, axis=0)
    inverse_count = 1.0 / (region_count * sub_count * row_count * feature_count)
    residual_norms = jnp.sqrt(total[:ITERS] * inverse_count + 1e-06)
    return adjoint, residual_norms


def solution(mesh):
    placed = (
        P(("region", "sub"), None),
        P(("region", "sub"), None),
        P(),
        P(("region", "sub"), None, None),
        P(("region", "sub")),
        P(("region", "sub")),
        P(("region", "sub"), None, None),
    )
    return jax.shard_map(
        local,
        mesh=mesh,
        in_specs=placed,
        out_specs=(P(("region", "sub"), None), P()),
        check_vma=False,
    )
```
